32 devices in a mesh: grp: 2 (over x), had: 16 (over z, y, core).
Axes of the slice: x: 2, y: 2, z: 4, core: 2. Of those that a mesh axis runs over, the one named last changes fastest.
Arguments:
- source_slabs: bfloat16 [512, 128, 128], P(('grp', 'had')), parts along dimension 0, may hold values from -6 to 6
- sink_slabs: bfloat16 [512, 128, 128], P(('grp', 'had')), parts along dimension 0, may hold values from -6 to 6
- perambulators: bfloat16 [4, 2, 128, 128], P('grp'), parts along dimension 0, may hold values from -0.5 to 0.5
- send_pick: int32 [32, 16], P(('grp', 'had')), parts along dimension 0, may hold values from 0 to 15
- graph_slot: int32 [32, 512, 2], P(('grp', 'had')), parts along dimension 0, may hold values from 0 to 15
- graph_sink: int32 [32, 512, 2], P(('grp', 'had')), parts along dimension 0, may hold values from 0 to 15
- graph_count: int32 [32], P(('grp', 'had')), parts along dimension 0, may hold values from 64 to 512, as said below
- pair_list: int32 [256, 2], P(('grp', 'had')), parts along dimension 0, may hold values from 0 to 15
Outputs:
- edge_matrices: bfloat16 [32, 128, 128], P(('grp', 'had')), parts along dimension 0
- pair_products: bfloat16 [256, 128, 128], P(('grp', 'had')), parts along dimension 0
The draws below stay inside these ranges and needn't reach their ends.
There are 2 independent parts, one for each index of `grp`. The reference program is written for one: setup_inputs(seed, part) draws one part's arguments, and reference() takes and returns one part's arrays. A program takes and returns all parts, laid end to end along the dimension named above; each array names one. Nothing has to cross between parts.
Inputs may be any that keep to these rules, and one draw needn't show every extreme that they name: Some reader uses all 512 graph slots; slots from graph_count on are unused.
All inputs are finite; a program needn't handle non-finite values.
Results may differ from the reference program's by a relative error of at most 0.012.
Values may be sent and summed in bfloat16 or wider, within the bound.
No kernel may reach another device: no remote copies, remote signals or barrier semaphores. Data moves between devices by JAX's collectives and lax.ppermute only.
A program may use at most 64 MiB of HBM per device.

```python
import math
import jax
import jax.numpy as jnp
from jax import lax

EVECS = 128
SLAB_DEV = 16
GRAPH_DEV = 512
READERS = 16
SLABS = 256
TSLICES = 2
PAIRS = 128


def draw_graph_count(key, part):
    shift_key, top_key = jax.random.split(jax.random.fold_in(key, 17))
    levels = jnp.array([GRAPH_DEV, GRAPH_DEV // 2, GRAPH_DEV // 4, GRAPH_DEV // 8], dtype=jnp.int32)
    chosen = levels[jax.random.randint(shift_key, (READERS,), 0, 4)]
    busiest = jax.random.randint(top_key, (), 0, READERS)
    return jnp.where(jnp.arange(READERS) == busiest, GRAPH_DEV, chosen).astype(jnp.int32)


def with_ends(drawn, own_key, smallest, top_value):
    dims = drawn.shape
    place = [jax.random.randint(jax.random.fold_in(own_key, axis), (), 0, dims[axis]) for axis in range(len(dims))]
    drawn = drawn.at[tuple(place)].set(smallest)
    longest = dims.index(max(dims))
    place[longest] = (place[longest] + 1) % dims[longest]
    return drawn.at[tuple(place)].set(top_value)


def block_scale(key, shape, cuts, least, top_value):
    gain = 1.0
    for position, shards_of in cuts:
        heights = jax.random.uniform(jax.random.fold_in(jax.random.fold_in(key, 6), position), (shards_of,), jnp.float32, least / len(cuts), top_value / len(cuts))
        gain = gain * jnp.repeat(jnp.exp(heights), shape[position] // shards_of).reshape((-1,) + (1,) * (len(shape) - 1 - position))
    return gain


def centred(own_key, dims, width, limit, shards=(), kind=jnp.bfloat16):
    level = block_scale(own_key, dims, shards, -0.22, 0.18) if shards else 1.0
    values = jax.random.normal(own_key, dims, jnp.float32) * width * level
    return jnp.minimum(jnp.maximum(values, -limit), limit).astype(kind)


def setup_inputs(seed: int = 0, part: int = 0) -> dict:
    key_of = jax.random.split(jax.random.key(seed), 9)
    part_splits = jax.random.split(jax.random.fold_in(key_of[8], part), 9)
    source_slabs = centred(part_splits[0], (SLABS, EVECS, EVECS), 1.0, 6.0, ((0, 16),))
    sink_slabs = centred(part_splits[1], (SLABS, EVECS, EVECS), 1.0, 6.0, ((0, 16),))
    perambulators = centred(part_splits[2], (TSLICES, 2, EVECS, EVECS), EVECS ** -0.5, 0.5)
    send_pick = with_ends(jax.random.randint(part_splits[3], (READERS, READERS), 0, SLAB_DEV), jax.random.fold_in(part_splits[3], 1), 0, SLAB_DEV - 1).astype(jnp.int32)
    graph_slot = with_ends(jax.random.randint(part_splits[4], (READERS, GRAPH_DEV, 2), 0, READERS), jax.random.fold_in(part_splits[4], 1), 0, READERS - 1).astype(jnp.int32)
    graph_sink = with_ends(jax.random.randint(part_splits[5], (READERS, GRAPH_DEV, 2), 0, SLAB_DEV), jax.random.fold_in(part_splits[5], 1), 0, SLAB_DEV - 1).astype(jnp.int32)
    graph_count = draw_graph_count(jax.random.fold_in(jax.random.fold_in(key_of[8], part), 71), part)
    pair_list = with_ends(jax.random.randint(part_splits[7], (PAIRS, 2), 0, READERS), jax.random.fold_in(part_splits[7], 1), 0, READERS - 1).astype(jnp.int32)
    return dict(source_slabs=source_slabs, sink_slabs=sink_slabs, perambulators=perambulators, send_pick=send_pick, graph_slot=graph_slot, graph_sink=graph_sink, graph_count=graph_count, pair_list=pair_list)


def rotated_slabs(source_slabs, perambulators):
    grouped = source_slabs.reshape(TSLICES, EVECS, EVECS, EVECS).astype(jnp.float32)
    first_turn = jnp.einsum('txa,tcab->tcxb', perambulators[:, 0].astype(jnp.float32), grouped).astype(jnp.bfloat16)
    second_turn = jnp.einsum('tcxb,tyb->tcxy', first_turn.astype(jnp.float32), perambulators[:, 1].astype(jnp.float32))
    return second_turn.astype(jnp.bfloat16).reshape(SLABS, EVECS, EVECS)

def reference(source_slabs, sink_slabs, perambulators, send_pick, graph_slot, graph_sink, graph_count, pair_list):
    rotated = rotated_slabs(source_slabs, perambulators)
    root_scale = 1.0 / math.sqrt(EVECS)
    edge_scale = 1.0 / math.sqrt(EVECS * GRAPH_DEV)
    owners = jnp.arange(READERS, dtype=jnp.int32)

    def reader_edge(packed):
        reader, slot_rows, sink_rows, graph_total = packed
        pick_column = lax.dynamic_index_in_dim(send_pick, reader, 1, keepdims=False)
        received = rotated[(owners * SLAB_DEV + pick_column).astype(jnp.int32)]
        resident = lax.dynamic_slice_in_dim(sink_slabs, (reader * SLAB_DEV).astype(jnp.int32), SLAB_DEV, 0)

        def factor(slots, sinks):
            product = jnp.einsum('gxb,gab->gxa', resident[sinks].astype(jnp.float32), received[slots].astype(jnp.float32))
            return (product * root_scale).astype(jnp.bfloat16)
        is_valid = (jnp.arange(GRAPH_DEV, dtype=jnp.int32) < graph_total).astype(jnp.float32)
        left_side = factor(slot_rows[:, 0], sink_rows[:, 0]).astype(jnp.float32) * is_valid[:, None, None]
        right_side = factor(slot_rows[:, 1], sink_rows[:, 1]).astype(jnp.float32)
        summed = jnp.einsum('gxa,gay->xy', left_side, right_side)
        return (summed * edge_scale).astype(jnp.bfloat16)
    edge_matrices = lax.map(reader_edge, (owners, graph_slot, graph_sink, graph_count))
    left_edges = edge_matrices[pair_list[:, 0]].astype(jnp.float32)
    right_edges = edge_matrices[pair_list[:, 1]].astype(jnp.float32)
    pair_products = (jnp.einsum('pxa,pay->pxy', left_edges, right_edges) * root_scale).astype(jnp.bfloat16)
    return (edge_matrices, pair_products)
```

```python
import functools
import math

import jax
import jax.numpy as jnp
from jax import lax
from jax.experimental import pallas as pl
from jax.experimental.pallas import tpu as pltpu
from jax.sharding import PartitionSpec as P

BF16 = jnp.bfloat16
F32 = jnp.float32
VMEM = pl.BlockSpec(memory_space=pltpu.VMEM)
SMEM = pl.BlockSpec(memory_space=pltpu.SMEM)
HBM = pl.BlockSpec(memory_space=pltpu.HBM)


def times_transposed(left, right):
    return lax.dot_general(left, right, (((1,), (1,)), ((), ())), preferred_element_type=F32)


def rotate_kernel(pick_hbm, source_hbm, peram_hbm, out_ref, pick_ref, source_ref, peram_ref, rotated_ref, sems):
    per_device, evecs, _ = source_ref.shape
    readers = out_ref.shape[0]
    timeslice = lax.axis_index("had") * per_device // evecs
    copies = [
        pltpu.make_async_copy(peram_hbm.at[timeslice], peram_ref, sems.at[0]),
        pltpu.make_async_copy(source_hbm, source_ref, sems.at[1]),
        pltpu.make_async_copy(pick_hbm, pick_ref, sems.at[2]),
    ]
    for copy in copies:
        copy.start()
    for copy in copies:
        copy.wait()
    group = math.gcd(4, per_device)
    for j in range(0, per_device, group):
        side_by_side = jnp.concatenate([source_ref[j + i] for i in range(group)], axis=1)
        half = jnp.dot(peram_ref[0], side_by_side, preferred_element_type=F32).astype(BF16)
        stacked = jnp.concatenate(
            [half[:, i * evecs : (i + 1) * evecs] for i in range(group)], axis=0
        )
        rotated = times_transposed(stacked, peram_ref[1]).astype(BF16)
        rotated_ref[j : j + group] = rotated.reshape(group, evecs, evecs)

    def place(r, carry):
        out_ref[r] = rotated_ref[pick_ref[0, r]]
        return carry

    lax.fori_loop(0, readers, place, 0, unroll=min(readers, 16))


def edge_kernel(block, root_scale, edge_scale, count_ref, slot_ref, sink_ref, received_ref, resident_ref, out_ref, *factors):
    slots, evecs, _ = received_ref.shape
    sinks = resident_ref.shape[0]
    total = count_ref[0]

    if factors:
        (factor_ref,) = factors
        wide, tall = math.gcd(2, slots), math.gcd(4, sinks)
        for s in range(0, slots, wide):
            weights = received_ref[s : s + wide].reshape(wide * evecs, evecs)
            for k in range(0, sinks, tall):
                rows = resident_ref[k : k + tall].reshape(tall * evecs, evecs)
                product = (times_transposed(rows, weights) * root_scale).astype(BF16)
                for i in range(wide):
                    first = (s + i) * sinks + k
                    factor_ref[first : first + tall] = product[
                        :, i * evecs : (i + 1) * evecs
                    ].reshape(tall, evecs, evecs)
        factor_ref[slots * sinks] = jnp.zeros((evecs, evecs), BF16)

        def factor(side, g):
            row = slot_ref[side, g] * sinks + sink_ref[side, g]
            if side == 0:
                row = jnp.where(g < total, row, slots * sinks)
            return factor_ref[row]
    else:

        def factor(side, g):
            product = times_transposed(
                resident_ref[sink_ref[side, g]], received_ref[slot_ref[side, g]]
            ) * root_scale
            if side == 0:
                product = jnp.where(g < total, product, 0.0)
            return product.astype(BF16)

    def step(b, total_sum):
        base = b * block
        left = jnp.concatenate([factor(0, base + i) for i in range(block)], axis=1)
        right = jnp.concatenate([factor(1, base + i) for i in range(block)], axis=0)
        return total_sum + jnp.dot(left, right, preferred_element_type=F32)

    summed = lax.fori_loop(
        0, (total + block - 1) // block, step, jnp.zeros((evecs, evecs), F32)
    )
    out_ref[0] = (summed * edge_scale).astype(BF16)


def pair_kernel(scale, place, pair_ref, *refs):
    *parts, out_ref, edge_ref = refs
    first = 0
    for part in parts:
        edge_ref[first : first + part.shape[0]] = part[...]
        first += part.shape[0]
    for i in range(out_ref.shape[0]):
        product = jnp.dot(
            edge_ref[place(pair_ref[0, i])],
            edge_ref[place(pair_ref[1, i])],
            preferred_element_type=F32,
        )
        out_ref[i] = (product * scale).astype(BF16)


def xor_phases(readers):
    bits = readers.bit_length() - 1
    near = [[1 << b] for b in range(min(2, bits))]
    step = 1 << len(near)
    far = [[step * i for i in range(readers // step - 1, 0, -1)]]
    return [phase for phase in far + near[::-1] if phase]


def gather_edges(edge, readers):
    if readers & (readers - 1) or readers > 16:
        return [lax.all_gather(edge, "had", axis=0, tiled=True)], lambda r: r
    held, masks = edge, [0]
    for number, phase in enumerate(phases := xor_phases(readers)):
        arrived = [
            lax.ppermute(held, "had", [(d, d ^ mask) for d in range(readers)]) for mask in phase
        ]
        masks = masks + [m ^ mask for mask in phase for m in masks]
        parts = [held] + arrived
        if number < len(phases) - 1:
            held = jnp.concatenate(parts, axis=0)

    def place(reader):
        wanted = reader ^ lax.axis_index("had")
        found = jnp.int32(0)
        for position, mask in enumerate(masks):
            found = jnp.where(wanted == mask, position, found)
        return found

    return parts, place


def shards(
    readers,
    source_slabs,
    sink_slabs,
    perambulators,
    send_pick,
    graph_slot,
    graph_sink,
    graph_count,
    pair_list,
):
    per_device, evecs, _ = source_slabs.shape
    sinks = sink_slabs.shape[0]
    graphs = graph_slot.shape[1]
    pairs = pair_list.shape[0]
    slab = (evecs, evecs)

    outgoing = pl.pallas_call(
        rotate_kernel,
        out_shape=jax.ShapeDtypeStruct((readers,) + slab, BF16),
        in_specs=[HBM, HBM, HBM],
        out_specs=VMEM,
        scratch_shapes=[
            pltpu.SMEM((1, readers), jnp.int32),
            pltpu.VMEM((per_device,) + slab, BF16),
            pltpu.VMEM((2,) + slab, BF16),
            pltpu.VMEM((per_device,) + slab, BF16),
            pltpu.SemaphoreType.DMA((3,)),
        ],
        compiler_params=pltpu.CompilerParams(vmem_limit_bytes=24 << 20),
        name="rotate",
    )(send_pick, source_slabs, perambulators)
    received = lax.all_to_all(outgoing, "had", split_axis=0, concat_axis=0, tiled=True)

    root_scale = 1.0 / math.sqrt(evecs)
    edge_scale = 1.0 / math.sqrt(evecs * graphs)
    dense = readers * sinks <= graphs
    block = math.gcd(128 if dense else 8, graphs)
    edge = pl.pallas_call(
        functools.partial(edge_kernel, block, root_scale, edge_scale),
        out_shape=jax.ShapeDtypeStruct((1,) + slab, BF16),
        in_specs=[SMEM, SMEM, SMEM, VMEM, VMEM],
        out_specs=VMEM,
        scratch_shapes=[pltpu.VMEM((readers * sinks + 1,) + slab, BF16)] if dense else [],
        compiler_params=pltpu.CompilerParams(vmem_limit_bytes=32 << 20),
        name="edge",
    )(graph_count, graph_slot[0].T, graph_sink[0].T, received, sink_slabs)

    parts, place = gather_edges(edge, readers)
    pair_products = pl.pallas_call(
        functools.partial(pair_kernel, root_scale, place),
        out_shape=jax.ShapeDtypeStruct((pairs,) + slab, BF16),
        in_specs=[SMEM] + [VMEM] * len(parts),
        out_specs=VMEM,
        scratch_shapes=[pltpu.VMEM((readers,) + slab, BF16)],
        compiler_params=pltpu.CompilerParams(vmem_limit_bytes=24 << 20),
        name="pairs",
    )(pair_list.T, *parts)
    return edge, pair_products


def solution(mesh):
    return jax.shard_map(
        functools.partial(shards, mesh.shape["had"]),
        mesh=mesh,
        in_specs=(
            P(("grp", "had"), None, None),
            P(("grp", "had"), None, None),
            P("grp", None, None, None),
            P(("grp", "had"), None),
            P(("grp", "had"), None, None),
            P(("grp", "had"), None, None),
            P(("grp", "had")),
            P(("grp", "had"), None),
        ),
        out_specs=(P(("grp", "had"), None, None), P(("grp", "had"), None, None)),
        check_vma=False,
    )
```

```python
import functools
import math

import jax
import jax.numpy as jnp
from jax import lax
from jax.experimental import pallas as pl
from jax.experimental.pallas import tpu as pltpu
from jax.sharding import PartitionSpec as P

BF16 = jnp.bfloat16
F32 = jnp.float32
VMEM = pl.BlockSpec(memory_space=pltpu.VMEM)
SMEM = pl.BlockSpec(memory_space=pltpu.SMEM)
HBM = pl.BlockSpec(memory_space=pltpu.HBM)
ORDER = (1, 4, 6, 2, 5, 7, 3)
EARLY = 4


def params(mebibytes):
    return pltpu.CompilerParams(vmem_limit_bytes=mebibytes << 20)


def times_transposed(left, right):
    return lax.dot_general(left, right, (((1,), (1,)), ((), ())), preferred_element_type=F32)


def rotate_slabs(pick_hbm, source_hbm, peram_hbm, pick_ref, source_ref, peram_ref, rotated_ref, sems):
    per_device, evecs, _ = source_ref.shape
    timeslice = lax.axis_index("had") * per_device // evecs
    copies = [
        pltpu.make_async_copy(peram_hbm.at[timeslice], peram_ref, sems.at[0]),
        pltpu.make_async_copy(source_hbm, source_ref, sems.at[1]),
        pltpu.make_async_copy(pick_hbm, pick_ref, sems.at[2]),
    ]
    for copy in copies:
        copy.start()
    for copy in copies:
        copy.wait()
    group = math.gcd(4, per_device)
    for j in range(0, per_device, group):
        side_by_side = jnp.concatenate([source_ref[j + i] for i in range(group)], axis=1)
        half = jnp.dot(peram_ref[0], side_by_side, preferred_element_type=F32).astype(BF16)
        stacked = jnp.concatenate(
            [half[:, i * evecs : (i + 1) * evecs] for i in range(group)], axis=0
        )
        rotated = times_transposed(stacked, peram_ref[1]).astype(BF16)
        rotated_ref[j : j + group] = rotated.reshape(group, evecs, evecs)


def rotate_kernel(pick_hbm, source_hbm, peram_hbm, out_ref, *scratch):
    pick_ref, _, _, rotated_ref, _ = scratch
    rotate_slabs(pick_hbm, source_hbm, peram_hbm, *scratch)

    def place(r, carry):
        out_ref[r] = rotated_ref[pick_ref[0, r]]
        return carry

    lax.fori_loop(0, out_ref.shape[0], place, 0)


def rotate_pairs_kernel(
    pick_hbm, source_hbm, peram_hbm, sink_hbm, mine_ref, other_ref, resident_ref, *scratch
):
    *scratch, sink_sem = scratch
    pick_ref, _, _, rotated_ref, _ = scratch
    sinks_in = pltpu.make_async_copy(sink_hbm, resident_ref, sink_sem)
    sinks_in.start()
    rotate_slabs(pick_hbm, source_hbm, peram_hbm, *scratch)
    me = lax.axis_index("had")
    for i in range(mine_ref.shape[0]):
        other_ref[i] = rotated_ref[pick_ref[0, me ^ (2 * i + 1)]]
        mine_ref[i] = rotated_ref[pick_ref[0, me ^ (2 * i)]]
    sinks_in.wait()


def zip_kernel(mine_ref, got_ref, *out_refs):
    for i, out_ref in enumerate(out_refs):
        out_ref[0] = mine_ref[i]
        out_ref[1] = got_ref[i]


def fill_factors(factor_ref, resident_ref, weights, first_slot, root_scale):
    sinks, evecs, _ = resident_ref.shape
    wide, tall = weights.shape[0] // evecs, math.gcd(4, sinks)
    for k in range(0, sinks, tall):
        rows = resident_ref[k : k + tall].reshape(tall * evecs, evecs)
        product = (times_transposed(rows, weights) * root_scale).astype(BF16)
        for i in range(wide):
            first = (first_slot + i) * sinks + k
            factor_ref[first : first + tall] = product[
                :, i * evecs : (i + 1) * evecs
            ].reshape(tall, evecs, evecs)


def factor_kernel(root_scale, first_slots, resident_ref, *refs):
    *arrived, factor_ref = refs
    _, evecs, _ = resident_ref.shape
    for first_slot, ref in zip(first_slots, arrived):
        fill_factors(factor_ref, resident_ref, ref[...].reshape(-1, evecs), first_slot, root_scale)


def graph_sum(block, total, factor, evecs):
    def step(b, total_sum):
        base = b * block
        left = jnp.concatenate([factor(0, base + i) for i in range(block)], axis=1)
        right = jnp.concatenate([factor(1, base + i) for i in range(block)], axis=0)
        return total_sum + jnp.dot(left, right, preferred_element_type=F32)

    return lax.fori_loop(
        0, (total + block - 1) // block, step, jnp.zeros((evecs, evecs), F32)
    )


def masked_edge_kernel(
    block, root_scale, edge_scale, first_slots, count_ref, slot_hbm, sink_hbm, resident_ref, *refs
):
    *arrived, _, out_ref, factor_ref, slot_ref, sink_ref, sems = refs
    sinks, evecs, _ = resident_ref.shape
    copies = [
        pltpu.make_async_copy(slot_hbm, slot_ref, sems.at[0]),
        pltpu.make_async_copy(sink_hbm, sink_ref, sems.at[1]),
    ]
    for copy in copies:
        copy.start()
    for first_slot, ref in zip(first_slots, arrived):
        fill_factors(factor_ref, resident_ref, ref[...].reshape(-1, evecs), first_slot, root_scale)
    nothing = factor_ref.shape[0] - 1
    factor_ref[nothing] = jnp.zeros((evecs, evecs), BF16)
    for copy in copies:
        copy.wait()
    me = lax.axis_index("had")
    total = count_ref[0]

    def factor(side, g):
        row = (slot_ref[side, g] ^ me) * sinks + sink_ref[side, g]
        if side == 0:
            row = jnp.where(g < total, row, nothing)
        return factor_ref[row]

    out_ref[0] = (graph_sum(block, total, factor, evecs) * edge_scale).astype(BF16)


def edge_kernel(block, root_scale, edge_scale, count_ref, slot_ref, sink_ref, received_ref, resident_ref, out_ref, *factors):
    slots, evecs, _ = received_ref.shape
    sinks = resident_ref.shape[0]
    total = count_ref[0]

    if factors:
        (factor_ref,) = factors
        wide = math.gcd(2, slots)
        for s in range(0, slots, wide):
            weights = received_ref[s : s + wide].reshape(wide * evecs, evecs)
            fill_factors(factor_ref, resident_ref, weights, s, root_scale)
        factor_ref[slots * sinks] = jnp.zeros((evecs, evecs), BF16)

        def factor(side, g):
            row = slot_ref[side, g] * sinks + sink_ref[side, g]
            if side == 0:
                row = jnp.where(g < total, row, slots * sinks)
            return factor_ref[row]
    else:

        def factor(side, g):
            product = times_transposed(
                resident_ref[sink_ref[side, g]], received_ref[slot_ref[side, g]]
            ) * root_scale
            if side == 0:
                product = jnp.where(g < total, product, 0.0)
            return product.astype(BF16)

    out_ref[0] = (graph_sum(block, total, factor, evecs) * edge_scale).astype(BF16)


def pair_kernel(scale, place, pair_ref, *refs):
    *parts, out_hbm, edge_ref, product_ref, sems = refs
    first = 0
    for part in parts:
        edge_ref[first : first + part.shape[0]] = part[...]
        first += part.shape[0]
    copies = []
    for i in range(out_hbm.shape[0]):
        product = jnp.dot(
            edge_ref[place(pair_ref[0, i])],
            edge_ref[place(pair_ref[1, i])],
            preferred_element_type=F32,
        )
        product_ref[i] = (product * scale).astype(BF16)
        copies.append(pltpu.make_async_copy(product_ref.at[i], out_hbm.at[i], sems.at[i]))
        copies[-1].start()
    for copy in copies:
        copy.wait()


def xor_phases(readers):
    far = list(range(readers - 4, 0, -4))
    return [phase for phase in ([2] if readers > 2 else [], far, [1]) if phase]


def by_xor(readers):
    return 2 <= readers <= 16 and readers & (readers - 1) == 0


def xor_permute(array, readers, mask):
    return lax.ppermute(array, "had", [(d, d ^ mask) for d in range(readers)])


def gather_edges(edge, readers):
    if not by_xor(readers):
        return [lax.all_gather(edge, "had", axis=0, tiled=True)], lambda r: r
    held = edge
    for phase in xor_phases(readers):
        arrived = [xor_permute(held, readers, mask) for mask in phase]
        parts = [held] + arrived[::-1]
        if phase != [1]:
            held = jnp.concatenate(parts, axis=0)

    def place(reader):
        mask = reader ^ lax.axis_index("had")
        return (mask >> 1) + (mask & 1) * (readers // 2)

    return parts, place


def shards(
    readers,
    source_slabs,
    sink_slabs,
    perambulators,
    send_pick,
    graph_slot,
    graph_sink,
    graph_count,
    pair_list,
):
    per_device, evecs, _ = source_slabs.shape
    sinks = sink_slabs.shape[0]
    graphs = graph_slot.shape[1]
    pairs = pair_list.shape[0]
    slab = (evecs, evecs)

    root_scale = 1.0 / math.sqrt(evecs)
    edge_scale = 1.0 / math.sqrt(evecs * graphs)
    dense = readers * sinks <= graphs
    block = math.gcd(128 if dense else 8, graphs)
    rotate_args = [
        pltpu.with_memory_space_constraint(array, pltpu.HBM)
        for array in (send_pick, source_slabs, perambulators)
    ]
    rotate_scratch = [
        pltpu.SMEM((1, readers), jnp.int32),
        pltpu.VMEM((per_device,) + slab, BF16),
        pltpu.VMEM((2,) + slab, BF16),
        pltpu.VMEM((per_device,) + slab, BF16),
        pltpu.SemaphoreType.DMA((3,)),
    ]
    counts = (graph_count, graph_slot[0].T, graph_sink[0].T)

    if dense and by_xor(readers):
        half = readers // 2
        mine, other, resident = pl.pallas_call(
            rotate_pairs_kernel,
            out_shape=[
                pltpu.VMEM((half,) + slab, BF16),
                pltpu.VMEM((half,) + slab, BF16),
                pltpu.VMEM((sinks,) + slab, BF16),
            ],
            in_specs=[HBM] * 4,
            out_specs=[VMEM] * 3,
            scratch_shapes=rotate_scratch + [pltpu.SemaphoreType.DMA],
            compiler_params=params(16),
            name="rotate",
        )(*rotate_args, pltpu.with_memory_space_constraint(sink_slabs, pltpu.HBM))
        got = xor_permute(other, readers, 1)
        pairs_for = pl.pallas_call(
            zip_kernel,
            out_shape=[pltpu.VMEM((2,) + slab, BF16)] * half,
            in_specs=[VMEM] * 2,
            out_specs=[VMEM] * half,
            compiler_params=params(16),
            name="zip",
        )(mine, got)
        order = [i for i in ORDER if i < half]
        arrived = {0: pairs_for[0]}
        for i in order:
            arrived[i] = xor_permute(pairs_for[i], readers, 2 * i)
        early = [0] + order[:EARLY]
        late = order[EARLY:]
        rows = readers * sinks + 1
        factors = pl.pallas_call(
            functools.partial(factor_kernel, root_scale, [2 * i for i in early]),
            out_shape=pltpu.VMEM((rows,) + slab, BF16),
            in_specs=[VMEM] * (1 + len(early)),
            out_specs=VMEM,
            compiler_params=params(16),
            cost_estimate=pl.CostEstimate(
                flops=8 * len(early) * sinks * evecs**3, bytes_accessed=0, transcendentals=0
            ),
            name="factors",
        )(resident, *[arrived[i] for i in early])
        edge, _ = pl.pallas_call(
            functools.partial(
                masked_edge_kernel, block, root_scale, edge_scale, [2 * i for i in late]
            ),
            out_shape=[
                pltpu.VMEM((1,) + slab, BF16),
                pltpu.VMEM((rows,) + slab, BF16),
            ],
            in_specs=[SMEM, HBM, HBM] + [VMEM] * (2 + len(late)),
            out_specs=[VMEM] * 2,
            scratch_shapes=[
                pltpu.SMEM((2, graphs), jnp.int32),
                pltpu.SMEM((2, graphs), jnp.int32),
                pltpu.SemaphoreType.DMA((2,)),
            ],
            input_output_aliases={4 + len(late): 1},
            compiler_params=params(16),
            name="edge",
        )(*counts, resident, *[arrived[i] for i in late], factors)
    else:
        outgoing = pl.pallas_call(
            rotate_kernel,
            out_shape=jax.ShapeDtypeStruct((readers,) + slab, BF16),
            in_specs=[HBM] * 3,
            out_specs=VMEM,
            scratch_shapes=rotate_scratch,
            compiler_params=params(24),
            name="rotate",
        )(*rotate_args)
        received = lax.all_to_all(outgoing, "had", split_axis=0, concat_axis=0, tiled=True)
        edge = pl.pallas_call(
            functools.partial(edge_kernel, block, root_scale, edge_scale),
            out_shape=jax.ShapeDtypeStruct((1,) + slab, BF16),
            in_specs=[SMEM, SMEM, SMEM, VMEM, VMEM],
            out_specs=VMEM,
            scratch_shapes=[pltpu.VMEM((readers * sinks + 1,) + slab, BF16)] if dense else [],
            compiler_params=params(32),
            name="edge",
        )(*counts, received, sink_slabs)

    parts, place = gather_edges(edge, readers)
    pair_products = pl.pallas_call(
        functools.partial(pair_kernel, root_scale, place),
        out_shape=jax.ShapeDtypeStruct((pairs,) + slab, BF16),
        in_specs=[SMEM] + [VMEM] * len(parts),
        out_specs=HBM,
        scratch_shapes=[
            pltpu.VMEM((readers,) + slab, BF16),
            pltpu.VMEM((pairs,) + slab, BF16),
            pltpu.SemaphoreType.DMA((pairs,)),
        ],
        compiler_params=params(24),
        name="pairs",
    )(pair_list.T, *parts)
    return edge, pair_products


def solution(mesh):
    return jax.shard_map(
        functools.partial(shards, mesh.shape["had"]),
        mesh=mesh,
        in_specs=(
            P(("grp", "had"), None, None),
            P(("grp", "had"), None, None),
            P("grp", None, None, None),
            P(("grp", "had"), None),
            P(("grp", "had"), None, None),
            P(("grp", "had"), None, None),
            P(("grp", "had")),
            P(("grp", "had"), None),
        ),
        out_specs=(P(("grp", "had"), None, None), P(("grp", "had"), None, None)),
        check_vma=False,
    )
```

```python
import functools
import math

import jax
import jax.numpy as jnp
from jax import lax
from jax.experimental import pallas as pl
from jax.experimental.pallas import tpu as pltpu
from jax.sharding import PartitionSpec as P

BF16 = jnp.bfloat16
F32 = jnp.float32
VMEM = pl.BlockSpec(memory_space=pltpu.VMEM)
SMEM = pl.BlockSpec(memory_space=pltpu.SMEM)
HBM = pl.BlockSpec(memory_space=pltpu.HBM)
ORDER = (1, 4, 6, 2, 5, 7, 3)
EARLY = 4
STEP = 64
LANES = 128


def params(mebibytes):
    return pltpu.CompilerParams(vmem_limit_bytes=mebibytes << 20)


def times_transposed(left, right):
    return lax.dot_general(left, right, (((1,), (1,)), ((), ())), preferred_element_type=F32)


def rotate_slabs(pick_hbm, source_hbm, peram_hbm, pick_ref, source_ref, peram_ref, rotated_ref, sems):
    per_device, evecs, _ = source_ref.shape
    timeslice = lax.axis_index("had") * per_device // evecs
    copies = [
        pltpu.make_async_copy(peram_hbm.at[timeslice], peram_ref, sems.at[0]),
        pltpu.make_async_copy(source_hbm, source_ref, sems.at[1]),
        pltpu.make_async_copy(pick_hbm, pick_ref, sems.at[2]),
    ]
    for copy in copies:
        copy.start()
    for copy in copies:
        copy.wait()
    group = math.gcd(4, per_device)
    for j in range(0, per_device, group):
        side_by_side = jnp.concatenate([source_ref[j + i] for i in range(group)], axis=1)
        half = jnp.dot(peram_ref[0], side_by_side, preferred_element_type=F32).astype(BF16)
        stacked = jnp.concatenate(
            [half[:, i * evecs : (i + 1) * evecs] for i in range(group)], axis=0
        )
        rotated = times_transposed(stacked, peram_ref[1]).astype(BF16)
        rotated_ref[j : j + group] = rotated.reshape(group, evecs, evecs)


def rotate_kernel(pick_hbm, source_hbm, peram_hbm, out_ref, *scratch):
    pick_ref, _, _, rotated_ref, _ = scratch
    rotate_slabs(pick_hbm, source_hbm, peram_hbm, *scratch)

    def place(r, carry):
        out_ref[r] = rotated_ref[pick_ref[0, r]]
        return carry

    lax.fori_loop(0, out_ref.shape[0], place, 0)


def rotate_pairs_kernel(
    pick_hbm, source_hbm, peram_hbm, *refs
):
    later_hbm, (mine_ref, other_ref), later_refs = refs[:3], refs[3:5], refs[5:8]
    *scratch, later_sems = refs[8:]
    pick_ref, _, _, rotated_ref, _ = scratch
    later = [
        pltpu.make_async_copy(hbm, ref, later_sems.at[i])
        for i, (hbm, ref) in enumerate(zip(later_hbm, later_refs))
    ]
    for copy in later:
        copy.start()
    rotate_slabs(pick_hbm, source_hbm, peram_hbm, *scratch)
    me = lax.axis_index("had")
    for i in range(mine_ref.shape[0]):
        other_ref[i] = rotated_ref[pick_ref[0, me ^ (2 * i + 1)]]
        mine_ref[i] = rotated_ref[pick_ref[0, me ^ (2 * i)]]
    for copy in later:
        copy.wait()


def zip_kernel(mine_ref, got_ref, *out_refs):
    for i, out_ref in enumerate(out_refs):
        out_ref[0] = mine_ref[i]
        out_ref[1] = got_ref[i]


def fill_factors(factor_ref, resident_ref, weights, first_slot, root_scale):
    sinks, evecs, _ = resident_ref.shape
    wide, tall = weights.shape[0] // evecs, math.gcd(4, sinks)
    for k in range(0, sinks, tall):
        rows = resident_ref[k : k + tall].reshape(tall * evecs, evecs)
        product = (times_transposed(rows, weights) * root_scale).astype(BF16)
        for i in range(wide):
            first = (first_slot + i) * sinks + k
            factor_ref[first : first + tall] = product[
                :, i * evecs : (i + 1) * evecs
            ].reshape(tall, evecs, evecs)


def down(row):
    return jnp.transpose(jnp.broadcast_to(row, (LANES, row.shape[1])))


def plan_graphs(total, slots, sinks, early, readers, sinks_each, step):
    graphs = slots.shape[1]
    nothing = readers * sinks_each

    def is_early(slot):
        found = [(slot >> 1) == i for i in early]
        return functools.reduce(jnp.logical_or, found)

    lane = lax.broadcasted_iota(jnp.int32, (1, graphs), 1)
    valid = lane < total
    both = is_early(slots[0:1]) & is_early(slots[1:2])
    kind = jnp.where(valid, jnp.where(both, 0, 1), 2)
    key = ((kind * readers + slots[0:1]) * sinks_each + sinks[0:1]).astype(F32)
    key_down = down(key)
    at = lax.broadcasted_iota(jnp.int32, (graphs, LANES), 0)
    across = lax.broadcasted_iota(jnp.int32, (graphs, LANES), 1)

    ranks = []
    for c in range(0, graphs, LANES):
        same = (key_down == key[:, c : c + LANES]) & (at < across + c)
        ranks.append(jnp.sum(jnp.where(same, 1.0, 0.0), axis=0, keepdims=True))
    rank = jnp.concatenate(ranks, axis=1).astype(jnp.int32)
    second = valid & ((rank & 1) == 1)
    first = valid & ((rank & 1) == 0)
    opens = [jnp.where(first & (kind == i), 1.0, 0.0) for i in range(2)]
    opened = jnp.concatenate(opens + [jnp.zeros((14, graphs), F32)], axis=0).astype(BF16)
    ahead = []
    for c in range(0, graphs, LANES):
        before = jnp.where(at < across + c, 1.0, 0.0).astype(BF16)
        ahead.append(jnp.dot(opened, before, preferred_element_type=F32))
    ahead = jnp.concatenate(ahead, axis=1)
    blocks = [jnp.sum(o, axis=1, keepdims=True).astype(jnp.int32) for o in opens]
    late_start = ((blocks[0] + step - 1) // step * step).astype(F32)
    block = jnp.where(
        first, jnp.where(kind == 0, ahead[0:1], late_start + ahead[1:2]), -1.0
    )
    mark = (key * graphs + (rank >> 1).astype(F32) + 1.0) * 2.0 + jnp.where(second, 1.0, 0.0)
    block_down, mark_down = down(block), down(mark)

    ones = jnp.ones((1, graphs), F32)
    columns = [slots[1:2].astype(F32), sinks[1:2].astype(F32), ones]
    columns += [slots[0:1].astype(F32), sinks[0:1].astype(F32)]
    values = jnp.concatenate(columns + [jnp.zeros((11, graphs), F32)], axis=0).astype(BF16)
    tables = []
    for c in range(0, graphs + LANES, LANES):
        opener = block_down == (across[:1] + c).astype(F32)
        opener_mark = jnp.sum(jnp.where(opener, mark_down, 0.0), axis=0, keepdims=True)
        closer = mark_down == opener_mark + 1.0
        one = jnp.dot(values, jnp.where(opener, 1.0, 0.0).astype(BF16), preferred_element_type=F32)
        two = jnp.dot(values, jnp.where(closer, 1.0, 0.0).astype(BF16), preferred_element_type=F32)
        rows = [
            jnp.where(one[2:3] > 0.5, one[3:4] * sinks_each + one[4:5], nothing),
            jnp.where(one[2:3] > 0.5, one[0:1] * sinks_each + one[1:2], nothing),
            jnp.where(two[2:3] > 0.5, two[0:1] * sinks_each + two[1:2], nothing),
        ]
        counts = jnp.where(across[:1] == 0, blocks[0], blocks[1])
        rows = [row.astype(jnp.int32) for row in rows] + [counts]
        tables.append(jnp.concatenate(rows + [jnp.zeros((4, LANES), jnp.int32)], axis=0))
    return jnp.concatenate(tables, axis=1)


def add_blocks(total_sum, table_ref, factor_ref, start, stop, step):
    def body(b, total_sum):
        base = b * step
        left = jnp.concatenate([factor_ref[table_ref[0, base + i]] for i in range(step)], axis=1)
        right = jnp.concatenate(
            [
                jnp.concatenate(
                    [factor_ref[table_ref[1, base + i]], factor_ref[table_ref[2, base + i]]], axis=1
                )
                for i in range(step)
            ],
            axis=0,
        )
        return total_sum + jnp.dot(left, right, preferred_element_type=F32)

    return lax.fori_loop(start, stop, body, total_sum)


def steps_of(count, step):
    return (count + step - 1) // step


def plan_kernel(step, readers, sinks, early, count_ref, slot_ref, sink_ref, table_ref):
    me = lax.axis_index("had")
    table_ref[...] = plan_graphs(
        count_ref[0], slot_ref[...] ^ me, sink_ref[...], early, readers, sinks, step
    )


def early_kernel(step, root_scale, early, table_ref, resident_ref, *refs):
    *arrived, factor_ref, sum_ref, smem_ref, sem = refs
    _, evecs, _ = resident_ref.shape
    copy = pltpu.make_async_copy(table_ref, smem_ref, sem)
    copy.start()
    for i, ref in zip(early, arrived):
        fill_factors(factor_ref, resident_ref, ref[...].reshape(-1, evecs), 2 * i, root_scale)
    factor_ref[factor_ref.shape[0] - 1] = jnp.zeros((evecs, evecs), BF16)
    copy.wait()
    stop = steps_of(smem_ref[3, 0], step)
    sum_ref[...] = add_blocks(
        jnp.zeros((evecs, 2 * evecs), F32), smem_ref, factor_ref, 0, stop, step
    )


def late_kernel(step, root_scale, edge_scale, late, table_ref, sum_ref, resident_ref, *refs):
    *arrived, _, out_ref, factor_ref, smem_ref, sem = refs
    _, evecs, _ = resident_ref.shape
    copy = pltpu.make_async_copy(table_ref, smem_ref, sem)
    copy.start()
    for i, ref in zip(late, arrived):
        fill_factors(factor_ref, resident_ref, ref[...].reshape(-1, evecs), 2 * i, root_scale)
    copy.wait()
    start = steps_of(smem_ref[3, 0], step)
    stop = start + steps_of(smem_ref[3, 1], step)
    both = add_blocks(sum_ref[...], smem_ref, factor_ref, start, stop, step)
    out_ref[0] = ((both[:, :evecs] + both[:, evecs:]) * edge_scale).astype(BF16)


def graph_sum(block, total, factor, evecs):
    def step(b, total_sum):
        base = b * block
        left = jnp.concatenate([factor(0, base + i) for i in range(block)], axis=1)
        right = jnp.concatenate([factor(1, base + i) for i in range(block)], axis=0)
        return total_sum + jnp.dot(left, right, preferred_element_type=F32)

    return lax.fori_loop(
        0, (total + block - 1) // block, step, jnp.zeros((evecs, evecs), F32)
    )


def edge_kernel(block, root_scale, edge_scale, count_ref, slot_ref, sink_ref, received_ref, resident_ref, out_ref, *factors):
    slots, evecs, _ = received_ref.shape
    sinks = resident_ref.shape[0]
    total = count_ref[0]

    if factors:
        (factor_ref,) = factors
        wide = math.gcd(2, slots)
        for s in range(0, slots, wide):
            weights = received_ref[s : s + wide].reshape(wide * evecs, evecs)
            fill_factors(factor_ref, resident_ref, weights, s, root_scale)
        factor_ref[slots * sinks] = jnp.zeros((evecs, evecs), BF16)

        def factor(side, g):
            row = slot_ref[side, g] * sinks + sink_ref[side, g]
            if side == 0:
                row = jnp.where(g < total, row, slots * sinks)
            return factor_ref[row]
    else:

        def factor(side, g):
            product = times_transposed(
                resident_ref[sink_ref[side, g]], received_ref[slot_ref[side, g]]
            ) * root_scale
            if side == 0:
                product = jnp.where(g < total, product, 0.0)
            return product.astype(BF16)

    out_ref[0] = (graph_sum(block, total, factor, evecs) * edge_scale).astype(BF16)


def pair_kernel(scale, place, pair_ref, *refs):
    *parts, out_hbm, edge_ref, product_ref, sems = refs
    first = 0
    for part in parts:
        edge_ref[first : first + part.shape[0]] = part[...]
        first += part.shape[0]
    copies = []
    for i in range(out_hbm.shape[0]):
        product = jnp.dot(
            edge_ref[place(pair_ref[0, i])],
            edge_ref[place(pair_ref[1, i])],
            preferred_element_type=F32,
        )
        product_ref[i] = (product * scale).astype(BF16)
        copies.append(pltpu.make_async_copy(product_ref.at[i], out_hbm.at[i], sems.at[i]))
        copies[-1].start()
    for copy in copies:
        copy.wait()


def xor_phases(readers):
    far = list(range(readers - 4, 0, -4))
    return [phase for phase in ([2] if readers > 2 else [], far, [1]) if phase]


def by_xor(readers):
    return 2 <= readers <= 16 and readers & (readers - 1) == 0


def xor_permute(array, readers, mask):
    return lax.ppermute(array, "had", [(d, d ^ mask) for d in range(readers)])


def gather_edges(edge, readers):
    if not by_xor(readers):
        return [lax.all_gather(edge, "had", axis=0, tiled=True)], lambda r: r
    held = edge
    for phase in xor_phases(readers):
        arrived = [xor_permute(held, readers, mask) for mask in phase]
        parts = [held] + arrived[::-1]
        if phase != [1]:
            held = jnp.concatenate(parts, axis=0)

    def place(reader):
        mask = reader ^ lax.axis_index("had")
        return (mask >> 1) + (mask & 1) * (readers // 2)

    return parts, place


def shards(
    readers,
    source_slabs,
    sink_slabs,
    perambulators,
    send_pick,
    graph_slot,
    graph_sink,
    graph_count,
    pair_list,
):
    per_device, evecs, _ = source_slabs.shape
    sinks = sink_slabs.shape[0]
    graphs = graph_slot.shape[1]
    pairs = pair_list.shape[0]
    slab = (evecs, evecs)

    root_scale = 1.0 / math.sqrt(evecs)
    edge_scale = 1.0 / math.sqrt(evecs * graphs)
    dense = readers * sinks <= graphs
    block = math.gcd(128 if dense else 8, graphs)
    rotate_args = [
        pltpu.with_memory_space_constraint(array, pltpu.HBM)
        for array in (send_pick, source_slabs, perambulators)
    ]
    rotate_scratch = [
        pltpu.SMEM((1, readers), jnp.int32),
        pltpu.VMEM((per_device,) + slab, BF16),
        pltpu.VMEM((2,) + slab, BF16),
        pltpu.VMEM((per_device,) + slab, BF16),
        pltpu.SemaphoreType.DMA((3,)),
    ]
    counts = (graph_count, graph_slot[0].T, graph_sink[0].T)

    if dense and by_xor(readers) and graphs % LANES == 0:
        half = readers // 2
        mine, other, resident, slot_table, sink_table = pl.pallas_call(
            rotate_pairs_kernel,
            out_shape=[
                pltpu.VMEM((half,) + slab, BF16),
                pltpu.VMEM((half,) + slab, BF16),
                pltpu.VMEM((sinks,) + slab, BF16),
                pltpu.VMEM((2, graphs), jnp.int32),
                pltpu.VMEM((2, graphs), jnp.int32),
            ],
            in_specs=[HBM] * 6,
            out_specs=[VMEM] * 5,
            scratch_shapes=rotate_scratch + [pltpu.SemaphoreType.DMA((3,))],
            compiler_params=params(16),
            name="rotate",
        )(
            *rotate_args,
            *[
                pltpu.with_memory_space_constraint(array, pltpu.HBM)
                for array in (sink_slabs, *counts[1:])
            ],
        )
        got = xor_permute(other, readers, 1)
        pairs_for = pl.pallas_call(
            zip_kernel,
            out_shape=[pltpu.VMEM((2,) + slab, BF16)] * half,
            in_specs=[VMEM] * 2,
            out_specs=[VMEM] * half,
            compiler_params=params(16),
            name="zip",
        )(mine, got)
        order = [i for i in ORDER if i < half]
        arrived = {0: pairs_for[0]}
        for i in order:
            arrived[i] = xor_permute(pairs_for[i], readers, 2 * i)
        early = [0] + order[:EARLY]
        late = order[EARLY:]
        rows = readers * sinks + 1
        table = pl.pallas_call(
            functools.partial(plan_kernel, STEP, readers, sinks, early),
            out_shape=pltpu.VMEM((8, graphs + LANES), jnp.int32),
            in_specs=[SMEM, VMEM, VMEM],
            out_specs=VMEM,
            compiler_params=params(16),
            cost_estimate=pl.CostEstimate(flops=10**8, bytes_accessed=0, transcendentals=0),
            name="plan",
        )(graph_count, slot_table, sink_table)
        factors, early_sum = pl.pallas_call(
            functools.partial(early_kernel, STEP, root_scale, early),
            out_shape=[
                pltpu.VMEM((rows,) + slab, BF16),
                pltpu.VMEM((evecs, 2 * evecs), F32),
            ],
            in_specs=[VMEM] * (2 + len(early)),
            out_specs=[VMEM] * 2,
            scratch_shapes=[
                pltpu.SMEM((8, graphs + LANES), jnp.int32),
                pltpu.SemaphoreType.DMA,
            ],
            compiler_params=params(16),
            cost_estimate=pl.CostEstimate(
                flops=8 * len(early) * sinks * evecs**3, bytes_accessed=0, transcendentals=0
            ),
            name="early",
        )(table, resident, *[arrived[i] for i in early])
        edge, _ = pl.pallas_call(
            functools.partial(late_kernel, STEP, root_scale, edge_scale, late),
            out_shape=[
                pltpu.VMEM((1,) + slab, BF16),
                pltpu.VMEM((rows,) + slab, BF16),
            ],
            in_specs=[VMEM] * (4 + len(late)),
            out_specs=[VMEM] * 2,
            scratch_shapes=[
                pltpu.SMEM((8, graphs + LANES), jnp.int32),
                pltpu.SemaphoreType.DMA,
            ],
            input_output_aliases={3 + len(late): 1},
            compiler_params=params(16),
            name="edge",
        )(table, early_sum, resident, *[arrived[i] for i in late], factors)
    else:
        outgoing = pl.pallas_call(
            rotate_kernel,
            out_shape=jax.ShapeDtypeStruct((readers,) + slab, BF16),
            in_specs=[HBM] * 3,
            out_specs=VMEM,
            scratch_shapes=rotate_scratch,
            compiler_params=params(24),
            name="rotate",
        )(*rotate_args)
        received = lax.all_to_all(outgoing, "had", split_axis=0, concat_axis=0, tiled=True)
        edge = pl.pallas_call(
            functools.partial(edge_kernel, block, root_scale, edge_scale),
            out_shape=jax.ShapeDtypeStruct((1,) + slab, BF16),
            in_specs=[SMEM, SMEM, SMEM, VMEM, VMEM],
            out_specs=VMEM,
            scratch_shapes=[pltpu.VMEM((readers * sinks + 1,) + slab, BF16)] if dense else [],
            compiler_params=params(32),
            name="edge",
        )(*counts, received, sink_slabs)

    parts, place = gather_edges(edge, readers)
    pair_products = pl.pallas_call(
        functools.partial(pair_kernel, root_scale, place),
        out_shape=jax.ShapeDtypeStruct((pairs,) + slab, BF16),
        in_specs=[SMEM] + [VMEM] * len(parts),
        out_specs=HBM,
        scratch_shapes=[
            pltpu.VMEM((readers,) + slab, BF16),
            pltpu.VMEM((pairs,) + slab, BF16),
            pltpu.SemaphoreType.DMA((pairs,)),
        ],
        compiler_params=params(24),
        name="pairs",
    )(pair_list.T, *parts)
    return edge, pair_products


def solution(mesh):
    return jax.shard_map(
        functools.partial(shards, mesh.shape["had"]),
        mesh=mesh,
        in_specs=(
            P(("grp", "had"), None, None),
            P(("grp", "had"), None, None),
            P("grp", None, None, None),
            P(("grp", "had"), None),
            P(("grp", "had"), None, None),
            P(("grp", "had"), None, None),
            P(("grp", "had")),
            P(("grp", "had"), None),
        ),
        out_specs=(P(("grp", "had"), None, None), P(("grp", "had"), None, None)),
        check_vma=False,
    )
```

```python
import functools
import math

import jax
import jax.numpy as jnp
from jax import lax
from jax.experimental import pallas as pl
from jax.experimental.pallas import tpu as pltpu
from jax.sharding import PartitionSpec as P

BF16 = jnp.bfloat16
F32 = jnp.float32
VMEM = pl.BlockSpec(memory_space=pltpu.VMEM)
SMEM = pl.BlockSpec(memory_space=pltpu.SMEM)
HBM = pl.BlockSpec(memory_space=pltpu.HBM)
ORDER = (1, 4, 6, 2, 5, 7, 3)
EARLY = 4
STEP = 64
LANES = 128


def params(mebibytes):
    return pltpu.CompilerParams(vmem_limit_bytes=mebibytes << 20)


def times_transposed(left, right):
    return lax.dot_general(left, right, (((1,), (1,)), ((), ())), preferred_element_type=F32)


def rotate_slabs(pick_hbm, source_hbm, peram_hbm, pick_ref, source_ref, peram_ref, rotated_ref, sems, later=()):
    per_device, evecs, _ = source_ref.shape
    timeslice = lax.axis_index("had") * per_device // evecs
    copies = [
        pltpu.make_async_copy(peram_hbm.at[timeslice], peram_ref, sems.at[0]),
        pltpu.make_async_copy(source_hbm, source_ref, sems.at[1]),
        pltpu.make_async_copy(pick_hbm, pick_ref, sems.at[2]),
    ]
    for copy in [*copies, *later]:
        copy.start()
    for copy in copies:
        copy.wait()
    group = math.gcd(4, per_device)
    for j in range(0, per_device, group):
        side_by_side = jnp.concatenate([source_ref[j + i] for i in range(group)], axis=1)
        half = jnp.dot(peram_ref[0], side_by_side, preferred_element_type=F32).astype(BF16)
        stacked = jnp.concatenate(
            [half[:, i * evecs : (i + 1) * evecs] for i in range(group)], axis=0
        )
        rotated = times_transposed(stacked, peram_ref[1]).astype(BF16)
        rotated_ref[j : j + group] = rotated.reshape(group, evecs, evecs)


def rotate_kernel(pick_hbm, source_hbm, peram_hbm, out_ref, *scratch):
    pick_ref, _, _, rotated_ref, _ = scratch
    rotate_slabs(pick_hbm, source_hbm, peram_hbm, *scratch)

    def place(r, carry):
        out_ref[r] = rotated_ref[pick_ref[0, r]]
        return carry

    lax.fori_loop(0, out_ref.shape[0], place, 0)


def rotate_pairs_kernel(
    pick_hbm, source_hbm, peram_hbm, *refs
):
    later_hbm, (mine_ref, other_ref), later_refs = refs[:3], refs[3:5], refs[5:8]
    *scratch, later_sems = refs[8:]
    pick_ref, _, _, rotated_ref, _ = scratch
    later = [
        pltpu.make_async_copy(hbm, ref, later_sems.at[i])
        for i, (hbm, ref) in enumerate(zip(later_hbm, later_refs))
    ]
    rotate_slabs(pick_hbm, source_hbm, peram_hbm, *scratch, later=later)
    me = lax.axis_index("had")
    for i in range(mine_ref.shape[0]):
        other_ref[i] = rotated_ref[pick_ref[0, me ^ (2 * i + 1)]]
        mine_ref[i] = rotated_ref[pick_ref[0, me ^ (2 * i)]]
    for copy in later:
        copy.wait()


def zip_kernel(mine_ref, got_ref, _, *out_refs):
    for i, out_ref in enumerate(out_refs):
        out_ref[0] = mine_ref[i]
        out_ref[1] = got_ref[i]


def fill_factors(factor_ref, resident_ref, weights, first_slot, root_scale):
    sinks, evecs, _ = resident_ref.shape
    wide, tall = weights.shape[0] // evecs, math.gcd(4, sinks)
    for k in range(0, sinks, tall):
        rows = resident_ref[k : k + tall].reshape(tall * evecs, evecs)
        product = (times_transposed(rows, weights) * root_scale).astype(BF16)
        for i in range(wide):
            first = (first_slot + i) * sinks + k
            factor_ref[first : first + tall] = product[
                :, i * evecs : (i + 1) * evecs
            ].reshape(tall, evecs, evecs)


def down(row):
    return jnp.transpose(jnp.broadcast_to(row, (LANES, row.shape[1])))


def plan_graphs(total, slots, sinks, early, readers, sinks_each, step):
    graphs = slots.shape[1]
    nothing = readers * sinks_each

    def is_early(slot):
        found = [(slot >> 1) == i for i in early]
        return functools.reduce(jnp.logical_or, found)

    lane = lax.broadcasted_iota(jnp.int32, (1, graphs), 1)
    valid = lane < total
    both = is_early(slots[0:1]) & is_early(slots[1:2])
    kind = jnp.where(valid, jnp.where(both, 0, 1), 2)
    key = ((kind * readers + slots[0:1]) * sinks_each + sinks[0:1]).astype(F32)
    key_down = down(key)
    at = lax.broadcasted_iota(jnp.int32, (graphs, LANES), 0)
    across = lax.broadcasted_iota(jnp.int32, (graphs, LANES), 1)

    ranks = []
    for c in range(0, graphs, LANES):
        same = (key_down == key[:, c : c + LANES]) & (at < across + c)
        ranks.append(jnp.sum(jnp.where(same, 1.0, 0.0), axis=0, keepdims=True))
    rank = jnp.concatenate(ranks, axis=1).astype(jnp.int32)
    second = valid & ((rank & 1) == 1)
    first = valid & ((rank & 1) == 0)
    opens = [jnp.where(first & (kind == i), 1.0, 0.0) for i in range(2)]
    opened = jnp.concatenate(opens + [jnp.zeros((14, graphs), F32)], axis=0).astype(BF16)
    ahead = []
    for c in range(0, graphs, LANES):
        before = jnp.where(at < across + c, 1.0, 0.0).astype(BF16)
        ahead.append(jnp.dot(opened, before, preferred_element_type=F32))
    ahead = jnp.concatenate(ahead, axis=1)
    blocks = [jnp.sum(o, axis=1, keepdims=True).astype(jnp.int32) for o in opens]
    late_start = ((blocks[0] + step - 1) // step * step).astype(F32)
    block = jnp.where(
        first, jnp.where(kind == 0, ahead[0:1], late_start + ahead[1:2]), -1.0
    )
    mark = (key * graphs + (rank >> 1).astype(F32) + 1.0) * 2.0 + jnp.where(second, 1.0, 0.0)
    block_down, mark_down = down(block), down(mark)

    ones = jnp.ones((1, graphs), F32)
    columns = [slots[1:2].astype(F32), sinks[1:2].astype(F32), ones]
    columns += [slots[0:1].astype(F32), sinks[0:1].astype(F32)]
    values = jnp.concatenate(columns + [jnp.zeros((11, graphs), F32)], axis=0).astype(BF16)
    tables = []
    for c in range(0, graphs + LANES, LANES):
        opener = block_down == (across[:1] + c).astype(F32)
        opener_mark = jnp.sum(jnp.where(opener, mark_down, 0.0), axis=0, keepdims=True)
        closer = mark_down == opener_mark + 1.0
        one = jnp.dot(values, jnp.where(opener, 1.0, 0.0).astype(BF16), preferred_element_type=F32)
        two = jnp.dot(values, jnp.where(closer, 1.0, 0.0).astype(BF16), preferred_element_type=F32)
        rows = [
            jnp.where(one[2:3] > 0.5, one[3:4] * sinks_each + one[4:5], nothing),
            jnp.where(one[2:3] > 0.5, one[0:1] * sinks_each + one[1:2], nothing),
            jnp.where(two[2:3] > 0.5, two[0:1] * sinks_each + two[1:2], nothing),
        ]
        counts = jnp.where(across[:1] == 0, blocks[0], blocks[1])
        rows = [row.astype(jnp.int32) for row in rows] + [counts]
        tables.append(jnp.concatenate(rows + [jnp.zeros((4, LANES), jnp.int32)], axis=0))
    return jnp.concatenate(tables, axis=1)


def add_blocks(total_sum, table_ref, factor_ref, start, stop, step):
    def body(b, total_sum):
        base = b * step
        left = jnp.concatenate([factor_ref[table_ref[0, base + i]] for i in range(step)], axis=1)
        right = jnp.concatenate(
            [
                jnp.concatenate(
                    [factor_ref[table_ref[1, base + i]], factor_ref[table_ref[2, base + i]]], axis=1
                )
                for i in range(step)
            ],
            axis=0,
        )
        return total_sum + jnp.dot(left, right, preferred_element_type=F32)

    return lax.fori_loop(start, stop, body, total_sum)


def steps_of(count, step):
    return (count + step - 1) // step


def plan_kernel(step, readers, sinks, early, count_ref, slot_ref, sink_ref, table_ref):
    me = lax.axis_index("had")
    table_ref[...] = plan_graphs(
        count_ref[0], slot_ref[...] ^ me, sink_ref[...], early, readers, sinks, step
    )


def early_kernel(step, root_scale, early, table_ref, resident_ref, *refs):
    *arrived, factor_ref, sum_ref, smem_ref, sem = refs
    _, evecs, _ = resident_ref.shape
    copy = pltpu.make_async_copy(table_ref, smem_ref, sem)
    copy.start()
    for i, ref in zip(early, arrived):
        fill_factors(factor_ref, resident_ref, ref[...].reshape(-1, evecs), 2 * i, root_scale)
    factor_ref[factor_ref.shape[0] - 1] = jnp.zeros((evecs, evecs), BF16)
    copy.wait()
    stop = steps_of(smem_ref[3, 0], step)
    sum_ref[...] = add_blocks(
        jnp.zeros((evecs, 2 * evecs), F32), smem_ref, factor_ref, 0, stop, step
    )


def late_kernel(step, root_scale, edge_scale, late, table_ref, sum_ref, resident_ref, *refs):
    *arrived, _, out_ref, factor_ref, smem_ref, sem = refs
    _, evecs, _ = resident_ref.shape
    copy = pltpu.make_async_copy(table_ref, smem_ref, sem)
    copy.start()
    for i, ref in zip(late, arrived):
        fill_factors(factor_ref, resident_ref, ref[...].reshape(-1, evecs), 2 * i, root_scale)
    copy.wait()
    start = steps_of(smem_ref[3, 0], step)
    stop = start + steps_of(smem_ref[3, 1], step)
    both = add_blocks(sum_ref[...], smem_ref, factor_ref, start, stop, step)
    out_ref[0] = ((both[:, :evecs] + both[:, evecs:]) * edge_scale).astype(BF16)


def graph_sum(block, total, factor, evecs):
    def step(b, total_sum):
        base = b * block
        left = jnp.concatenate([factor(0, base + i) for i in range(block)], axis=1)
        right = jnp.concatenate([factor(1, base + i) for i in range(block)], axis=0)
        return total_sum + jnp.dot(left, right, preferred_element_type=F32)

    return lax.fori_loop(
        0, (total + block - 1) // block, step, jnp.zeros((evecs, evecs), F32)
    )


def edge_kernel(block, root_scale, edge_scale, count_ref, slot_ref, sink_ref, received_ref, resident_ref, out_ref, *factors):
    slots, evecs, _ = received_ref.shape
    sinks = resident_ref.shape[0]
    total = count_ref[0]

    if factors:
        (factor_ref,) = factors
        wide = math.gcd(2, slots)
        for s in range(0, slots, wide):
            weights = received_ref[s : s + wide].reshape(wide * evecs, evecs)
            fill_factors(factor_ref, resident_ref, weights, s, root_scale)
        factor_ref[slots * sinks] = jnp.zeros((evecs, evecs), BF16)

        def factor(side, g):
            row = slot_ref[side, g] * sinks + sink_ref[side, g]
            if side == 0:
                row = jnp.where(g < total, row, slots * sinks)
            return factor_ref[row]
    else:

        def factor(side, g):
            product = times_transposed(
                resident_ref[sink_ref[side, g]], received_ref[slot_ref[side, g]]
            ) * root_scale
            if side == 0:
                product = jnp.where(g < total, product, 0.0)
            return product.astype(BF16)

    out_ref[0] = (graph_sum(block, total, factor, evecs) * edge_scale).astype(BF16)


def pair_kernel(scale, place, pair_ref, *refs):
    *parts, out_hbm, edge_ref, product_ref, sems = refs
    first = 0
    for part in parts:
        edge_ref[first : first + part.shape[0]] = part[...]
        first += part.shape[0]
    copies = []
    for i in range(out_hbm.shape[0]):
        product = jnp.dot(
            edge_ref[place(pair_ref[0, i])],
            edge_ref[place(pair_ref[1, i])],
            preferred_element_type=F32,
        )
        product_ref[i] = (product * scale).astype(BF16)
        copies.append(pltpu.make_async_copy(product_ref.at[i], out_hbm.at[i], sems.at[i]))
        copies[-1].start()
    for copy in copies:
        copy.wait()


def xor_phases(readers):
    far = list(range(readers - 4, 0, -4))
    return [phase for phase in ([2] if readers > 2 else [], far, [1]) if phase]


def by_xor(readers):
    return 2 <= readers <= 16 and readers & (readers - 1) == 0


def xor_permute(array, readers, mask):
    return lax.ppermute(array, "had", [(d, d ^ mask) for d in range(readers)])


def gather_edges(edge, readers):
    if not by_xor(readers):
        return [lax.all_gather(edge, "had", axis=0, tiled=True)], lambda r: r
    held = edge
    for phase in xor_phases(readers):
        arrived = [xor_permute(held, readers, mask) for mask in phase]
        parts = [held] + arrived[::-1]
        if phase != [1]:
            held = jnp.concatenate(parts, axis=0)

    def place(reader):
        mask = reader ^ lax.axis_index("had")
        return (mask >> 1) + (mask & 1) * (readers // 2)

    return parts, place


def shards(
    readers,
    source_slabs,
    sink_slabs,
    perambulators,
    send_pick,
    graph_slot,
    graph_sink,
    graph_count,
    pair_list,
):
    per_device, evecs, _ = source_slabs.shape
    sinks = sink_slabs.shape[0]
    graphs = graph_slot.shape[1]
    pairs = pair_list.shape[0]
    slab = (evecs, evecs)

    root_scale = 1.0 / math.sqrt(evecs)
    edge_scale = 1.0 / math.sqrt(evecs * graphs)
    dense = readers * sinks <= graphs
    block = math.gcd(128 if dense else 8, graphs)
    rotate_args = [
        pltpu.with_memory_space_constraint(array, pltpu.HBM)
        for array in (send_pick, source_slabs, perambulators)
    ]
    rotate_scratch = [
        pltpu.SMEM((1, readers), jnp.int32),
        pltpu.VMEM((per_device,) + slab, BF16),
        pltpu.VMEM((2,) + slab, BF16),
        pltpu.VMEM((per_device,) + slab, BF16),
        pltpu.SemaphoreType.DMA((3,)),
    ]
    counts = (graph_count, graph_slot[0].T, graph_sink[0].T)

    if dense and by_xor(readers) and graphs % LANES == 0:
        half = readers // 2
        mine, other, resident, slot_table, sink_table = pl.pallas_call(
            rotate_pairs_kernel,
            out_shape=[
                pltpu.VMEM((half,) + slab, BF16),
                pltpu.VMEM((half,) + slab, BF16),
                pltpu.VMEM((sinks,) + slab, BF16),
                pltpu.VMEM((2, graphs), jnp.int32),
                pltpu.VMEM((2, graphs), jnp.int32),
            ],
            in_specs=[HBM] * 6,
            out_specs=[VMEM] * 5,
            scratch_shapes=rotate_scratch + [pltpu.SemaphoreType.DMA((3,))],
            compiler_params=params(16),
            name="rotate",
        )(
            *rotate_args,
            *[
                pltpu.with_memory_space_constraint(array, pltpu.HBM)
                for array in (sink_slabs, *counts[1:])
            ],
        )
        got = xor_permute(other, readers, 1)
        order = [i for i in ORDER if i < half]
        early = [0] + order[:EARLY]
        late = order[EARLY:]
        table = pl.pallas_call(
            functools.partial(plan_kernel, STEP, readers, sinks, early),
            out_shape=pltpu.VMEM((8, graphs + LANES), jnp.int32),
            in_specs=[SMEM, VMEM, VMEM],
            out_specs=VMEM,
            compiler_params=params(16),
            cost_estimate=pl.CostEstimate(flops=10**8, bytes_accessed=0, transcendentals=0),
            name="plan",
        )(graph_count, slot_table, sink_table)
        pairs_for = pl.pallas_call(
            zip_kernel,
            out_shape=[pltpu.VMEM((2,) + slab, BF16)] * half,
            in_specs=[VMEM] * 3,
            out_specs=[VMEM] * half,
            compiler_params=params(16),
            name="zip",
        )(mine, got, table)
        arrived = {0: pairs_for[0]}
        for i in order:
            arrived[i] = xor_permute(pairs_for[i], readers, 2 * i)
        rows = readers * sinks + 1
        factors, early_sum = pl.pallas_call(
            functools.partial(early_kernel, STEP, root_scale, early),
            out_shape=[
                pltpu.VMEM((rows,) + slab, BF16),
                pltpu.VMEM((evecs, 2 * evecs), F32),
            ],
            in_specs=[VMEM] * (2 + len(early)),
            out_specs=[VMEM] * 2,
            scratch_shapes=[
                pltpu.SMEM((8, graphs + LANES), jnp.int32),
                pltpu.SemaphoreType.DMA,
            ],
            compiler_params=params(16),
            cost_estimate=pl.CostEstimate(
                flops=8 * len(early) * sinks * evecs**3, bytes_accessed=0, transcendentals=0
            ),
            name="early",
        )(table, resident, *[arrived[i] for i in early])
        edge, _ = pl.pallas_call(
            functools.partial(late_kernel, STEP, root_scale, edge_scale, late),
            out_shape=[
                pltpu.VMEM((1,) + slab, BF16),
                pltpu.VMEM((rows,) + slab, BF16),
            ],
            in_specs=[VMEM] * (4 + len(late)),
            out_specs=[VMEM] * 2,
            scratch_shapes=[
                pltpu.SMEM((8, graphs + LANES), jnp.int32),
                pltpu.SemaphoreType.DMA,
            ],
            input_output_aliases={3 + len(late): 1},
            compiler_params=params(16),
            name="edge",
        )(table, early_sum, resident, *[arrived[i] for i in late], factors)
    else:
        outgoing = pl.pallas_call(
            rotate_kernel,
            out_shape=jax.ShapeDtypeStruct((readers,) + slab, BF16),
            in_specs=[HBM] * 3,
            out_specs=VMEM,
            scratch_shapes=rotate_scratch,
            compiler_params=params(24),
            name="rotate",
        )(*rotate_args)
        received = lax.all_to_all(outgoing, "had", split_axis=0, concat_axis=0, tiled=True)
        edge = pl.pallas_call(
            functools.partial(edge_kernel, block, root_scale, edge_scale),
            out_shape=jax.ShapeDtypeStruct((1,) + slab, BF16),
            in_specs=[SMEM, SMEM, SMEM, VMEM, VMEM],
            out_specs=VMEM,
            scratch_shapes=[pltpu.VMEM((readers * sinks + 1,) + slab, BF16)] if dense else [],
            compiler_params=params(32),
            name="edge",
        )(*counts, received, sink_slabs)

    parts, place = gather_edges(edge, readers)
    pair_products = pl.pallas_call(
        functools.partial(pair_kernel, root_scale, place),
        out_shape=jax.ShapeDtypeStruct((pairs,) + slab, BF16),
        in_specs=[SMEM] + [VMEM] * len(parts),
        out_specs=HBM,
        scratch_shapes=[
            pltpu.VMEM((readers,) + slab, BF16),
            pltpu.VMEM((pairs,) + slab, BF16),
            pltpu.SemaphoreType.DMA((pairs,)),
        ],
        compiler_params=params(24),
        name="pairs",
    )(pair_list.T, *parts)
    return edge, pair_products


def solution(mesh):
    return jax.shard_map(
        functools.partial(shards, mesh.shape["had"]),
        mesh=mesh,
        in_specs=(
            P(("grp", "had"), None, None),
            P(("grp", "had"), None, None),
            P("grp", None, None, None),
            P(("grp", "had"), None),
            P(("grp", "had"), None, None),
            P(("grp", "had"), None, None),
            P(("grp", "had")),
            P(("grp", "had"), None),
        ),
        out_specs=(P(("grp", "had"), None, None), P(("grp", "had"), None, None)),
        check_vma=False,
    )
```

```python
import functools
import math

import jax
import jax.numpy as jnp
from jax import lax
from jax.experimental import pallas as pl
from jax.experimental.pallas import tpu as pltpu
from jax.sharding import PartitionSpec as P

BF16 = jnp.bfloat16
F32 = jnp.float32
VMEM = pl.BlockSpec(memory_space=pltpu.VMEM)
SMEM = pl.BlockSpec(memory_space=pltpu.SMEM)
HBM = pl.BlockSpec(memory_space=pltpu.HBM)
ORDER = (1, 4, 6, 2, 5, 7, 3)
EARLY = 4
STEP = 64
LANES = 128


def params(mebibytes):
    return pltpu.CompilerParams(vmem_limit_bytes=mebibytes << 20)


def times_transposed(left, right):
    return lax.dot_general(left, right, (((1,), (1,)), ((), ())), preferred_element_type=F32)


def rotate_slabs(pick_hbm, source_hbm, peram_hbm, pick_ref, source_ref, peram_ref, rotated_ref, sems, later=()):
    per_device, evecs, _ = source_ref.shape
    timeslice = lax.axis_index("had") * per_device // evecs
    copies = [
        pltpu.make_async_copy(peram_hbm.at[timeslice], peram_ref, sems.at[0]),
        pltpu.make_async_copy(source_hbm, source_ref, sems.at[1]),
        pltpu.make_async_copy(pick_hbm, pick_ref, sems.at[2]),
    ]
    for copy in [*copies, *later]:
        copy.start()
    for copy in copies:
        copy.wait()
    group = math.gcd(4, per_device)
    for j in range(0, per_device, group):
        side_by_side = jnp.concatenate([source_ref[j + i] for i in range(group)], axis=1)
        half = jnp.dot(peram_ref[0], side_by_side, preferred_element_type=F32).astype(BF16)
        stacked = jnp.concatenate(
            [half[:, i * evecs : (i + 1) * evecs] for i in range(group)], axis=0
        )
        rotated = times_transposed(stacked, peram_ref[1]).astype(BF16)
        rotated_ref[j : j + group] = rotated.reshape(group, evecs, evecs)


def rotate_kernel(pick_hbm, source_hbm, peram_hbm, out_ref, *scratch):
    pick_ref, _, _, rotated_ref, _ = scratch
    rotate_slabs(pick_hbm, source_hbm, peram_hbm, *scratch)

    def place(r, carry):
        out_ref[r] = rotated_ref[pick_ref[0, r]]
        return carry

    lax.fori_loop(0, out_ref.shape[0], place, 0)


def rotate_pairs_kernel(
    pick_hbm, source_hbm, peram_hbm, *refs
):
    later_hbm, (mine_ref, other_ref), later_refs = refs[:3], refs[3:5], refs[5:8]
    *scratch, later_sems = refs[8:]
    pick_ref, _, _, rotated_ref, _ = scratch
    later = [
        pltpu.make_async_copy(hbm, ref, later_sems.at[i])
        for i, (hbm, ref) in enumerate(zip(later_hbm, later_refs))
    ]
    rotate_slabs(pick_hbm, source_hbm, peram_hbm, *scratch, later=later)
    me = lax.axis_index("had")
    for i in range(mine_ref.shape[0]):
        other_ref[i] = rotated_ref[pick_ref[0, me ^ (2 * i + 1)]]
        mine_ref[i] = rotated_ref[pick_ref[0, me ^ (2 * i)]]
    for copy in later:
        copy.wait()


def zip_kernel(mine_ref, got_ref, _, *out_refs):
    for i, out_ref in enumerate(out_refs):
        out_ref[0] = mine_ref[i]
        out_ref[1] = got_ref[i]


def fill_factors(factor_ref, resident_ref, weights, first_slot, root_scale):
    sinks, evecs, _ = resident_ref.shape
    wide, tall = weights.shape[0] // evecs, math.gcd(4, sinks)
    for k in range(0, sinks, tall):
        rows = resident_ref[k : k + tall].reshape(tall * evecs, evecs)
        product = (times_transposed(rows, weights) * root_scale).astype(BF16)
        for i in range(wide):
            first = (first_slot + i) * sinks + k
            factor_ref[first : first + tall] = product[
                :, i * evecs : (i + 1) * evecs
            ].reshape(tall, evecs, evecs)


def down(row):
    return jnp.transpose(jnp.broadcast_to(row, (LANES, row.shape[1])))


def plan_graphs(total, slots, sinks, early, readers, sinks_each, step):
    graphs = slots.shape[1]
    nothing = readers * sinks_each

    def is_early(slot):
        found = [(slot >> 1) == i for i in early]
        return functools.reduce(jnp.logical_or, found)

    lane = lax.broadcasted_iota(jnp.int32, (1, graphs), 1)
    valid = lane < total
    both = is_early(slots[0:1]) & is_early(slots[1:2])
    kind = jnp.where(valid, jnp.where(both, 0, 1), 2)
    key = ((kind * readers + slots[0:1]) * sinks_each + sinks[0:1]).astype(F32)
    key_down = down(key)
    at = lax.broadcasted_iota(jnp.int32, (graphs, LANES), 0)
    across = lax.broadcasted_iota(jnp.int32, (graphs, LANES), 1)

    ranks = []
    for c in range(0, graphs, LANES):
        same = (key_down == key[:, c : c + LANES]) & (at < across + c)
        ranks.append(jnp.sum(jnp.where(same, 1.0, 0.0), axis=0, keepdims=True))
    rank = jnp.concatenate(ranks, axis=1).astype(jnp.int32)
    second = valid & ((rank & 1) == 1)
    first = valid & ((rank & 1) == 0)
    opens = [jnp.where(first & (kind == i), 1.0, 0.0) for i in range(2)]
    opened = jnp.concatenate(opens + [jnp.zeros((14, graphs), F32)], axis=0).astype(BF16)
    ahead = []
    for c in range(0, graphs, LANES):
        before = jnp.where(at < across + c, 1.0, 0.0).astype(BF16)
        ahead.append(jnp.dot(opened, before, preferred_element_type=F32))
    ahead = jnp.concatenate(ahead, axis=1)
    blocks = [jnp.sum(o, axis=1, keepdims=True).astype(jnp.int32) for o in opens]
    late_start = ((blocks[0] + step - 1) // step * step).astype(F32)
    block = jnp.where(
        first, jnp.where(kind == 0, ahead[0:1], late_start + ahead[1:2]), -1.0
    )
    mark = (key * graphs + (rank >> 1).astype(F32) + 1.0) * 2.0 + jnp.where(second, 1.0, 0.0)
    block_down, mark_down = down(block), down(mark)

    ones = jnp.ones((1, graphs), F32)
    columns = [slots[1:2].astype(F32), sinks[1:2].astype(F32), ones]
    columns += [slots[0:1].astype(F32), sinks[0:1].astype(F32)]
    values = jnp.concatenate(columns + [jnp.zeros((11, graphs), F32)], axis=0).astype(BF16)
    tables = []
    for c in range(0, graphs + LANES, LANES):
        opener = block_down == (across[:1] + c).astype(F32)
        opener_mark = jnp.sum(jnp.where(opener, mark_down, 0.0), axis=0, keepdims=True)
        closer = mark_down == opener_mark + 1.0
        one = jnp.dot(values, jnp.where(opener, 1.0, 0.0).astype(BF16), preferred_element_type=F32)
        two = jnp.dot(values, jnp.where(closer, 1.0, 0.0).astype(BF16), preferred_element_type=F32)
        rows = [
            jnp.where(one[2:3] > 0.5, one[3:4] * sinks_each + one[4:5], nothing),
            jnp.where(one[2:3] > 0.5, one[0:1] * sinks_each + one[1:2], nothing),
            jnp.where(two[2:3] > 0.5, two[0:1] * sinks_each + two[1:2], nothing),
        ]
        counts = jnp.where(across[:1] == 0, blocks[0], blocks[1])
        rows = [row.astype(jnp.int32) for row in rows] + [counts]
        tables.append(jnp.concatenate(rows + [jnp.zeros((4, LANES), jnp.int32)], axis=0))
    return jnp.concatenate(tables, axis=1)


def add_blocks(total_sum, table_ref, factor_ref, start, stop, step):
    def body(b, total_sum):
        base = b * step
        left = jnp.concatenate([factor_ref[table_ref[0, base + i]] for i in range(step)], axis=1)
        right = jnp.concatenate(
            [
                jnp.concatenate(
                    [factor_ref[table_ref[1, base + i]], factor_ref[table_ref[2, base + i]]], axis=1
                )
                for i in range(step)
            ],
            axis=0,
        )
        return total_sum + jnp.dot(left, right, preferred_element_type=F32)

    return lax.fori_loop(start, stop, body, total_sum)


def steps_of(count, step):
    return (count + step - 1) // step


def plan_kernel(step, readers, sinks, early, count_ref, slot_ref, sink_ref, table_ref):
    me = lax.axis_index("had")
    table_ref[...] = plan_graphs(
        count_ref[0], slot_ref[...] ^ me, sink_ref[...], early, readers, sinks, step
    )


def early_kernel(step, root_scale, early, table_ref, resident_ref, *refs):
    *arrived, factor_ref, sum_ref, smem_ref, sem = refs
    _, evecs, _ = resident_ref.shape
    copy = pltpu.make_async_copy(table_ref, smem_ref, sem)
    copy.start()
    for i, ref in zip(early, arrived):
        fill_factors(factor_ref, resident_ref, ref[...].reshape(-1, evecs), 2 * i, root_scale)
    factor_ref[factor_ref.shape[0] - 1] = jnp.zeros((evecs, evecs), BF16)
    copy.wait()
    stop = steps_of(smem_ref[3, 0], step)
    sum_ref[...] = add_blocks(
        jnp.zeros((evecs, 2 * evecs), F32), smem_ref, factor_ref, 0, stop, step
    )


def late_kernel(step, root_scale, edge_scale, late, table_ref, sum_ref, resident_ref, *refs):
    *arrived, _, out_ref, factor_ref, smem_ref, sem = refs
    _, evecs, _ = resident_ref.shape
    copy = pltpu.make_async_copy(table_ref, smem_ref, sem)
    copy.start()
    for i, ref in zip(late, arrived):
        fill_factors(factor_ref, resident_ref, ref[...].reshape(-1, evecs), 2 * i, root_scale)
    copy.wait()
    start = steps_of(smem_ref[3, 0], step)
    stop = start + steps_of(smem_ref[3, 1], step)
    both = add_blocks(sum_ref[...], smem_ref, factor_ref, start, stop, step)
    out_ref[0] = ((both[:, :evecs] + both[:, evecs:]) * edge_scale).astype(BF16)


def graph_sum(block, total, factor, evecs):
    def step(b, total_sum):
        base = b * block
        left = jnp.concatenate([factor(0, base + i) for i in range(block)], axis=1)
        right = jnp.concatenate([factor(1, base + i) for i in range(block)], axis=0)
        return total_sum + jnp.dot(left, right, preferred_element_type=F32)

    return lax.fori_loop(
        0, (total + block - 1) // block, step, jnp.zeros((evecs, evecs), F32)
    )


def edge_kernel(block, root_scale, edge_scale, count_ref, slot_ref, sink_ref, received_ref, resident_ref, out_ref, *factors):
    slots, evecs, _ = received_ref.shape
    sinks = resident_ref.shape[0]
    total = count_ref[0]

    if factors:
        (factor_ref,) = factors
        wide = math.gcd(2, slots)
        for s in range(0, slots, wide):
            weights = received_ref[s : s + wide].reshape(wide * evecs, evecs)
            fill_factors(factor_ref, resident_ref, weights, s, root_scale)
        factor_ref[slots * sinks] = jnp.zeros((evecs, evecs), BF16)

        def factor(side, g):
            row = slot_ref[side, g] * sinks + sink_ref[side, g]
            if side == 0:
                row = jnp.where(g < total, row, slots * sinks)
            return factor_ref[row]
    else:

        def factor(side, g):
            product = times_transposed(
                resident_ref[sink_ref[side, g]], received_ref[slot_ref[side, g]]
            ) * root_scale
            if side == 0:
                product = jnp.where(g < total, product, 0.0)
            return product.astype(BF16)

    out_ref[0] = (graph_sum(block, total, factor, evecs) * edge_scale).astype(BF16)


def pair_kernel(scale, place, pair_ref, *refs):
    *parts, out_hbm, edge_ref, product_ref, sems = refs
    first = 0
    for part in parts:
        edge_ref[first : first + part.shape[0]] = part[...]
        first += part.shape[0]
    copies = []
    for i in range(out_hbm.shape[0]):
        product = jnp.dot(
            edge_ref[place(pair_ref[0, i])],
            edge_ref[place(pair_ref[1, i])],
            preferred_element_type=F32,
        )
        product_ref[i] = (product * scale).astype(BF16)
        copies.append(pltpu.make_async_copy(product_ref.at[i], out_hbm.at[i], sems.at[i]))
        copies[-1].start()
    for copy in copies:
        copy.wait()


def xor_phases(readers):
    far = [4 * z + 1 for z in range(readers // 4 - 1, 0, -1)]
    return [phase for phase in (far, [3] if readers > 2 else [], [1]) if phase]


def by_xor(readers):
    return 2 <= readers <= 16 and readers & (readers - 1) == 0


def xor_permute(array, readers, mask):
    return lax.ppermute(array, "had", [(d, d ^ mask) for d in range(readers)])


def gather_edges(edge, readers):
    if not by_xor(readers):
        return [lax.all_gather(edge, "had", axis=0, tiled=True)], lambda r: r
    held = edge
    for phase in xor_phases(readers):
        arrived = {mask: xor_permute(held, readers, mask) for mask in phase}
        parts = [held] + [arrived[mask] for mask in sorted(phase)]
        if phase != [1]:
            held = jnp.concatenate(parts, axis=0)

    def place(reader):
        mask = reader ^ lax.axis_index("had")
        other_core = mask ^ (mask >> 1) ^ jnp.where(mask >= 4, 1, 0)
        return (
            (mask >> 2) + ((mask >> 1) & 1) * (readers // 4) + (other_core & 1) * (readers // 2)
        )

    return parts, place


def shards(
    readers,
    source_slabs,
    sink_slabs,
    perambulators,
    send_pick,
    graph_slot,
    graph_sink,
    graph_count,
    pair_list,
):
    per_device, evecs, _ = source_slabs.shape
    sinks = sink_slabs.shape[0]
    graphs = graph_slot.shape[1]
    pairs = pair_list.shape[0]
    slab = (evecs, evecs)

    root_scale = 1.0 / math.sqrt(evecs)
    edge_scale = 1.0 / math.sqrt(evecs * graphs)
    dense = readers * sinks <= graphs
    block = math.gcd(128 if dense else 8, graphs)
    rotate_args = [
        pltpu.with_memory_space_constraint(array, pltpu.HBM)
        for array in (send_pick, source_slabs, perambulators)
    ]
    rotate_scratch = [
        pltpu.SMEM((1, readers), jnp.int32),
        pltpu.VMEM((per_device,) + slab, BF16),
        pltpu.VMEM((2,) + slab, BF16),
        pltpu.VMEM((per_device,) + slab, BF16),
        pltpu.SemaphoreType.DMA((3,)),
    ]
    counts = (graph_count, graph_slot[0].T, graph_sink[0].T)

    if dense and by_xor(readers) and graphs % LANES == 0:
        half = readers // 2
        mine, other, resident, slot_table, sink_table = pl.pallas_call(
            rotate_pairs_kernel,
            out_shape=[
                pltpu.VMEM((half,) + slab, BF16),
                pltpu.VMEM((half,) + slab, BF16),
                pltpu.VMEM((sinks,) + slab, BF16),
                pltpu.VMEM((2, graphs), jnp.int32),
                pltpu.VMEM((2, graphs), jnp.int32),
            ],
            in_specs=[HBM] * 6,
            out_specs=[VMEM] * 5,
            scratch_shapes=rotate_scratch + [pltpu.SemaphoreType.DMA((3,))],
            compiler_params=params(16),
            name="rotate",
        )(
            *rotate_args,
            *[
                pltpu.with_memory_space_constraint(array, pltpu.HBM)
                for array in (sink_slabs, *counts[1:])
            ],
        )
        got = xor_permute(other, readers, 1)
        order = [i for i in ORDER if i < half]
        early = [0] + order[:EARLY]
        late = order[EARLY:]
        table = pl.pallas_call(
            functools.partial(plan_kernel, STEP, readers, sinks, early),
            out_shape=pltpu.VMEM((8, graphs + LANES), jnp.int32),
            in_specs=[SMEM, VMEM, VMEM],
            out_specs=VMEM,
            compiler_params=params(16),
            cost_estimate=pl.CostEstimate(flops=10**8, bytes_accessed=0, transcendentals=0),
            name="plan",
        )(graph_count, slot_table, sink_table)
        pairs_for = pl.pallas_call(
            zip_kernel,
            out_shape=[pltpu.VMEM((2,) + slab, BF16)] * half,
            in_specs=[VMEM] * 3,
            out_specs=[VMEM] * half,
            compiler_params=params(16),
            name="zip",
        )(mine, got, table)
        arrived = {0: pairs_for[0]}
        for i in order:
            arrived[i] = xor_permute(pairs_for[i], readers, 2 * i)
        rows = readers * sinks + 1
        factors, early_sum = pl.pallas_call(
            functools.partial(early_kernel, STEP, root_scale, early),
            out_shape=[
                pltpu.VMEM((rows,) + slab, BF16),
                pltpu.VMEM((evecs, 2 * evecs), F32),
            ],
            in_specs=[VMEM] * (2 + len(early)),
            out_specs=[VMEM] * 2,
            scratch_shapes=[
                pltpu.SMEM((8, graphs + LANES), jnp.int32),
                pltpu.SemaphoreType.DMA,
            ],
            compiler_params=params(16),
            cost_estimate=pl.CostEstimate(
                flops=8 * len(early) * sinks * evecs**3, bytes_accessed=0, transcendentals=0
            ),
            name="early",
        )(table, resident, *[arrived[i] for i in early])
        edge, _ = pl.pallas_call(
            functools.partial(late_kernel, STEP, root_scale, edge_scale, late),
            out_shape=[
                pltpu.VMEM((1,) + slab, BF16),
                pltpu.VMEM((rows,) + slab, BF16),
            ],
            in_specs=[VMEM] * (4 + len(late)),
            out_specs=[VMEM] * 2,
            scratch_shapes=[
                pltpu.SMEM((8, graphs + LANES), jnp.int32),
                pltpu.SemaphoreType.DMA,
            ],
            input_output_aliases={3 + len(late): 1},
            compiler_params=params(16),
            name="edge",
        )(table, early_sum, resident, *[arrived[i] for i in late], factors)
    else:
        outgoing = pl.pallas_call(
            rotate_kernel,
            out_shape=jax.ShapeDtypeStruct((readers,) + slab, BF16),
            in_specs=[HBM] * 3,
            out_specs=VMEM,
            scratch_shapes=rotate_scratch,
            compiler_params=params(24),
            name="rotate",
        )(*rotate_args)
        received = lax.all_to_all(outgoing, "had", split_axis=0, concat_axis=0, tiled=True)
        edge = pl.pallas_call(
            functools.partial(edge_kernel, block, root_scale, edge_scale),
            out_shape=jax.ShapeDtypeStruct((1,) + slab, BF16),
            in_specs=[SMEM, SMEM, SMEM, VMEM, VMEM],
            out_specs=VMEM,
            scratch_shapes=[pltpu.VMEM((readers * sinks + 1,) + slab, BF16)] if dense else [],
            compiler_params=params(32),
            name="edge",
        )(*counts, received, sink_slabs)

    parts, place = gather_edges(edge, readers)
    pair_products = pl.pallas_call(
        functools.partial(pair_kernel, root_scale, place),
        out_shape=jax.ShapeDtypeStruct((pairs,) + slab, BF16),
        in_specs=[SMEM] + [VMEM] * len(parts),
        out_specs=HBM,
        scratch_shapes=[
            pltpu.VMEM((readers,) + slab, BF16),
            pltpu.VMEM((pairs,) + slab, BF16),
            pltpu.SemaphoreType.DMA((pairs,)),
        ],
        compiler_params=params(24),
        name="pairs",
    )(pair_list.T, *parts)
    return edge, pair_products


def solution(mesh):
    return jax.shard_map(
        functools.partial(shards, mesh.shape["had"]),
        mesh=mesh,
        in_specs=(
            P(("grp", "had"), None, None),
            P(("grp", "had"), None, None),
            P("grp", None, None, None),
            P(("grp", "had"), None),
            P(("grp", "had"), None, None),
            P(("grp", "had"), None, None),
            P(("grp", "had")),
            P(("grp", "had"), None),
        ),
        out_specs=(P(("grp", "had"), None, None), P(("grp", "had"), None, None)),
        check_vma=False,
    )
```

```python
import functools
import math

import jax
import jax.numpy as jnp
from jax import lax
from jax.experimental import pallas as pl
from jax.experimental.pallas import tpu as pltpu
from jax.sharding import PartitionSpec as P

BF16 = jnp.bfloat16
F32 = jnp.float32
VMEM = pl.BlockSpec(memory_space=pltpu.VMEM)
SMEM = pl.BlockSpec(memory_space=pltpu.SMEM)
HBM = pl.BlockSpec(memory_space=pltpu.HBM)
ORDER = (1, 4, 6, 2, 5, 7, 3)
EARLY = 4
STEP = 32
WIDE = 2
LANES = 128


def params(mebibytes):
    return pltpu.CompilerParams(vmem_limit_bytes=mebibytes << 20)


def times_transposed(left, right):
    return lax.dot_general(left, right, (((1,), (1,)), ((), ())), preferred_element_type=F32)


def rotate_slabs(pick_hbm, source_hbm, peram_hbm, pick_ref, source_ref, peram_ref, rotated_ref, sems, later=()):
    per_device, evecs, _ = source_ref.shape
    timeslice = lax.axis_index("had") * per_device // evecs
    copies = [
        pltpu.make_async_copy(peram_hbm.at[timeslice], peram_ref, sems.at[0]),
        pltpu.make_async_copy(source_hbm, source_ref, sems.at[1]),
        pltpu.make_async_copy(pick_hbm, pick_ref, sems.at[2]),
    ]
    for copy in [*copies, *later]:
        copy.start()
    for copy in copies:
        copy.wait()
    group = math.gcd(4, per_device)
    for j in range(0, per_device, group):
        side_by_side = jnp.concatenate([source_ref[j + i] for i in range(group)], axis=1)
        half = jnp.dot(peram_ref[0], side_by_side, preferred_element_type=F32).astype(BF16)
        stacked = jnp.concatenate(
            [half[:, i * evecs : (i + 1) * evecs] for i in range(group)], axis=0
        )
        rotated = times_transposed(stacked, peram_ref[1]).astype(BF16)
        rotated_ref[j : j + group] = rotated.reshape(group, evecs, evecs)


def rotate_kernel(pick_hbm, source_hbm, peram_hbm, out_ref, *scratch):
    pick_ref, _, _, rotated_ref, _ = scratch
    rotate_slabs(pick_hbm, source_hbm, peram_hbm, *scratch)

    def place(r, carry):
        out_ref[r] = rotated_ref[pick_ref[0, r]]
        return carry

    lax.fori_loop(0, out_ref.shape[0], place, 0)


def rotate_pairs_kernel(
    pick_hbm, source_hbm, peram_hbm, *refs
):
    later_hbm, (mine_ref, other_ref), later_refs = refs[:3], refs[3:5], refs[5:8]
    *scratch, later_sems = refs[8:]
    pick_ref, _, _, rotated_ref, _ = scratch
    later = [
        pltpu.make_async_copy(hbm, ref, later_sems.at[i])
        for i, (hbm, ref) in enumerate(zip(later_hbm, later_refs))
    ]
    rotate_slabs(pick_hbm, source_hbm, peram_hbm, *scratch, later=later)
    me = lax.axis_index("had")
    for i in range(mine_ref.shape[0]):
        other_ref[i] = rotated_ref[pick_ref[0, me ^ (2 * i + 1)]]
        mine_ref[i] = rotated_ref[pick_ref[0, me ^ (2 * i)]]
    for copy in later:
        copy.wait()


def zip_kernel(mine_ref, got_ref, _, *out_refs):
    for i, out_ref in enumerate(out_refs):
        out_ref[0] = mine_ref[i]
        out_ref[1] = got_ref[i]


def fill_factors(factor_ref, resident_ref, weights, first_slot, root_scale):
    sinks, evecs, _ = resident_ref.shape
    wide, tall = weights.shape[0] // evecs, math.gcd(4, sinks)
    for k in range(0, sinks, tall):
        rows = resident_ref[k : k + tall].reshape(tall * evecs, evecs)
        product = (times_transposed(rows, weights) * root_scale).astype(BF16)
        for i in range(wide):
            first = (first_slot + i) * sinks + k
            factor_ref[first : first + tall] = product[
                :, i * evecs : (i + 1) * evecs
            ].reshape(tall, evecs, evecs)


def down(row):
    return jnp.transpose(jnp.broadcast_to(row, (LANES, row.shape[1])))


def plan_graphs(total, slots, sinks, early, readers, sinks_each, step):
    graphs = slots.shape[1]
    nothing = readers * sinks_each

    def is_early(slot):
        found = [(slot >> 1) == i for i in early]
        return functools.reduce(jnp.logical_or, found)

    lane = lax.broadcasted_iota(jnp.int32, (1, graphs), 1)
    valid = lane < total
    both = is_early(slots[0:1]) & is_early(slots[1:2])
    kind = jnp.where(valid, jnp.where(both, 0, 1), 2)
    key = ((kind * readers + slots[0:1]) * sinks_each + sinks[0:1]).astype(F32)
    key_down = down(key)
    at = lax.broadcasted_iota(jnp.int32, (graphs, LANES), 0)
    across = lax.broadcasted_iota(jnp.int32, (graphs, LANES), 1)

    ranks = []
    for c in range(0, graphs, LANES):
        same = (key_down == key[:, c : c + LANES]) & (at < across + c)
        ranks.append(jnp.sum(jnp.where(same, 1.0, 0.0), axis=0, keepdims=True))
    rank = jnp.concatenate(ranks, axis=1).astype(jnp.int32)
    second = valid & ((rank & 1) == 1)
    first = valid & ((rank & 1) == 0)
    opens = [jnp.where(first & (kind == i), 1.0, 0.0) for i in range(2)]
    opened = jnp.concatenate(opens + [jnp.zeros((14, graphs), F32)], axis=0).astype(BF16)
    ahead = []
    for c in range(0, graphs, LANES):
        before = jnp.where(at < across + c, 1.0, 0.0).astype(BF16)
        ahead.append(jnp.dot(opened, before, preferred_element_type=F32))
    ahead = jnp.concatenate(ahead, axis=1)
    blocks = [jnp.sum(o, axis=1, keepdims=True).astype(jnp.int32) for o in opens]
    late_start = ((blocks[0] + step - 1) // step * step).astype(F32)
    block = jnp.where(
        first, jnp.where(kind == 0, ahead[0:1], late_start + ahead[1:2]), -1.0
    )
    mark = (key * graphs + (rank >> 1).astype(F32) + 1.0) * 2.0 + jnp.where(second, 1.0, 0.0)
    block_down, mark_down = down(block), down(mark)

    ones = jnp.ones((1, graphs), F32)
    columns = [slots[1:2].astype(F32), sinks[1:2].astype(F32), ones]
    columns += [slots[0:1].astype(F32), sinks[0:1].astype(F32)]
    values = jnp.concatenate(columns + [jnp.zeros((11, graphs), F32)], axis=0).astype(BF16)
    tables = []
    for c in range(0, graphs + LANES, LANES):
        opener = block_down == (across[:1] + c).astype(F32)
        opener_mark = jnp.sum(jnp.where(opener, mark_down, 0.0), axis=0, keepdims=True)
        closer = mark_down == opener_mark + 1.0
        one = jnp.dot(values, jnp.where(opener, 1.0, 0.0).astype(BF16), preferred_element_type=F32)
        two = jnp.dot(values, jnp.where(closer, 1.0, 0.0).astype(BF16), preferred_element_type=F32)
        rows = [
            jnp.where(one[2:3] > 0.5, one[3:4] * sinks_each + one[4:5], nothing),
            jnp.where(one[2:3] > 0.5, one[0:1] * sinks_each + one[1:2], nothing),
            jnp.where(two[2:3] > 0.5, two[0:1] * sinks_each + two[1:2], nothing),
        ]
        counts = jnp.where(across[:1] == 0, blocks[0], blocks[1])
        rows = [row.astype(jnp.int32) for row in rows] + [counts]
        tables.append(jnp.concatenate(rows + [jnp.zeros((4, LANES), jnp.int32)], axis=0))
    return jnp.concatenate(tables, axis=1)


def add_blocks(total_sum, table_ref, factor_ref, start, stop, step):
    def add(total_sum, base, blocks):
        left = jnp.concatenate([factor_ref[table_ref[0, base + i]] for i in range(blocks)], axis=1)
        right = jnp.concatenate(
            [
                jnp.concatenate(
                    [factor_ref[table_ref[1, base + i]], factor_ref[table_ref[2, base + i]]], axis=1
                )
                for i in range(blocks)
            ],
            axis=0,
        )
        return total_sum + jnp.dot(left, right, preferred_element_type=F32)

    wide = (stop - start) // WIDE
    total_sum = lax.fori_loop(
        0, wide, lambda b, t: add(t, (start + b * WIDE) * step, WIDE * step), total_sum
    )
    return lax.fori_loop(
        start + wide * WIDE, stop, lambda b, t: add(t, b * step, step), total_sum
    )


def steps_of(count, step):
    return (count + step - 1) // step


def plan_kernel(step, readers, sinks, early, count_ref, slot_ref, sink_ref, table_ref):
    me = lax.axis_index("had")
    table_ref[...] = plan_graphs(
        count_ref[0], slot_ref[...] ^ me, sink_ref[...], early, readers, sinks, step
    )


def early_kernel(step, root_scale, early, table_ref, resident_ref, *refs):
    *arrived, factor_ref, sum_ref, smem_ref, sem = refs
    _, evecs, _ = resident_ref.shape
    copy = pltpu.make_async_copy(table_ref, smem_ref, sem)
    copy.start()
    for i, ref in zip(early, arrived):
        fill_factors(factor_ref, resident_ref, ref[...].reshape(-1, evecs), 2 * i, root_scale)
    factor_ref[factor_ref.shape[0] - 1] = jnp.zeros((evecs, evecs), BF16)
    copy.wait()
    stop = steps_of(smem_ref[3, 0], step)
    sum_ref[...] = add_blocks(
        jnp.zeros((evecs, 2 * evecs), F32), smem_ref, factor_ref, 0, stop, step
    )


def late_kernel(step, root_scale, edge_scale, late, table_ref, sum_ref, resident_ref, *refs):
    *arrived, _, out_ref, factor_ref, smem_ref, sem = refs
    _, evecs, _ = resident_ref.shape
    copy = pltpu.make_async_copy(table_ref, smem_ref, sem)
    copy.start()
    for i, ref in zip(late, arrived):
        fill_factors(factor_ref, resident_ref, ref[...].reshape(-1, evecs), 2 * i, root_scale)
    copy.wait()
    start = steps_of(smem_ref[3, 0], step)
    stop = start + steps_of(smem_ref[3, 1], step)
    both = add_blocks(sum_ref[...], smem_ref, factor_ref, start, stop, step)
    out_ref[0] = ((both[:, :evecs] + both[:, evecs:]) * edge_scale).astype(BF16)


def graph_sum(block, total, factor, evecs):
    def step(b, total_sum):
        base = b * block
        left = jnp.concatenate([factor(0, base + i) for i in range(block)], axis=1)
        right = jnp.concatenate([factor(1, base + i) for i in range(block)], axis=0)
        return total_sum + jnp.dot(left, right, preferred_element_type=F32)

    return lax.fori_loop(
        0, (total + block - 1) // block, step, jnp.zeros((evecs, evecs), F32)
    )


def edge_kernel(block, root_scale, edge_scale, count_ref, slot_ref, sink_ref, received_ref, resident_ref, out_ref, *factors):
    slots, evecs, _ = received_ref.shape
    sinks = resident_ref.shape[0]
    total = count_ref[0]

    if factors:
        (factor_ref,) = factors
        wide = math.gcd(2, slots)
        for s in range(0, slots, wide):
            weights = received_ref[s : s + wide].reshape(wide * evecs, evecs)
            fill_factors(factor_ref, resident_ref, weights, s, root_scale)
        factor_ref[slots * sinks] = jnp.zeros((evecs, evecs), BF16)

        def factor(side, g):
            row = slot_ref[side, g] * sinks + sink_ref[side, g]
            if side == 0:
                row = jnp.where(g < total, row, slots * sinks)
            return factor_ref[row]
    else:

        def factor(side, g):
            product = times_transposed(
                resident_ref[sink_ref[side, g]], received_ref[slot_ref[side, g]]
            ) * root_scale
            if side == 0:
                product = jnp.where(g < total, product, 0.0)
            return product.astype(BF16)

    out_ref[0] = (graph_sum(block, total, factor, evecs) * edge_scale).astype(BF16)


def pair_kernel(scale, place, pair_ref, *refs):
    *parts, out_hbm, edge_ref, product_ref, sems = refs
    first = 0
    for part in parts:
        edge_ref[first : first + part.shape[0]] = part[...]
        first += part.shape[0]
    copies = []
    for i in range(out_hbm.shape[0]):
        product = jnp.dot(
            edge_ref[place(pair_ref[0, i])],
            edge_ref[place(pair_ref[1, i])],
            preferred_element_type=F32,
        )
        product_ref[i] = (product * scale).astype(BF16)
        copies.append(pltpu.make_async_copy(product_ref.at[i], out_hbm.at[i], sems.at[i]))
        copies[-1].start()
    for copy in copies:
        copy.wait()


def xor_phases(readers):
    far = [4 * z + 1 for z in range(readers // 4 - 1, 0, -1)]
    return [phase for phase in (far, [3] if readers > 2 else [], [1]) if phase]


def by_xor(readers):
    return 2 <= readers <= 16 and readers & (readers - 1) == 0


def xor_permute(array, readers, mask):
    return lax.ppermute(array, "had", [(d, d ^ mask) for d in range(readers)])


def gather_edges(edge, readers):
    if not by_xor(readers):
        return [lax.all_gather(edge, "had", axis=0, tiled=True)], lambda r: r
    held = edge
    for phase in xor_phases(readers):
        arrived = {mask: xor_permute(held, readers, mask) for mask in phase}
        parts = [held] + [arrived[mask] for mask in sorted(phase)]
        if phase != [1]:
            held = jnp.concatenate(parts, axis=0)

    def place(reader):
        mask = reader ^ lax.axis_index("had")
        other_core = mask ^ (mask >> 1) ^ jnp.where(mask >= 4, 1, 0)
        return (
            (mask >> 2) + ((mask >> 1) & 1) * (readers // 4) + (other_core & 1) * (readers // 2)
        )

    return parts, place


def shards(
    readers,
    source_slabs,
    sink_slabs,
    perambulators,
    send_pick,
    graph_slot,
    graph_sink,
    graph_count,
    pair_list,
):
    per_device, evecs, _ = source_slabs.shape
    sinks = sink_slabs.shape[0]
    graphs = graph_slot.shape[1]
    pairs = pair_list.shape[0]
    slab = (evecs, evecs)

    root_scale = 1.0 / math.sqrt(evecs)
    edge_scale = 1.0 / math.sqrt(evecs * graphs)
    dense = readers * sinks <= graphs
    block = math.gcd(128 if dense else 8, graphs)
    rotate_args = [
        pltpu.with_memory_space_constraint(array, pltpu.HBM)
        for array in (send_pick, source_slabs, perambulators)
    ]
    rotate_scratch = [
        pltpu.SMEM((1, readers), jnp.int32),
        pltpu.VMEM((per_device,) + slab, BF16),
        pltpu.VMEM((2,) + slab, BF16),
        pltpu.VMEM((per_device,) + slab, BF16),
        pltpu.SemaphoreType.DMA((3,)),
    ]
    counts = (graph_count, graph_slot[0].T, graph_sink[0].T)

    if dense and by_xor(readers) and graphs % LANES == 0:
        half = readers // 2
        mine, other, resident, slot_table, sink_table = pl.pallas_call(
            rotate_pairs_kernel,
            out_shape=[
                pltpu.VMEM((half,) + slab, BF16),
                pltpu.VMEM((half,) + slab, BF16),
                pltpu.VMEM((sinks,) + slab, BF16),
                pltpu.VMEM((2, graphs), jnp.int32),
                pltpu.VMEM((2, graphs), jnp.int32),
            ],
            in_specs=[HBM] * 6,
            out_specs=[VMEM] * 5,
            scratch_shapes=rotate_scratch + [pltpu.SemaphoreType.DMA((3,))],
            compiler_params=params(16),
            name="rotate",
        )(
            *rotate_args,
            *[
                pltpu.with_memory_space_constraint(array, pltpu.HBM)
                for array in (sink_slabs, *counts[1:])
            ],
        )
        got = xor_permute(other, readers, 1)
        order = [i for i in ORDER if i < half]
        early = [0] + order[:EARLY]
        late = order[EARLY:]
        table = pl.pallas_call(
            functools.partial(plan_kernel, STEP, readers, sinks, early),
            out_shape=pltpu.VMEM((8, graphs + LANES), jnp.int32),
            in_specs=[SMEM, VMEM, VMEM],
            out_specs=VMEM,
            compiler_params=params(16),
            cost_estimate=pl.CostEstimate(flops=10**8, bytes_accessed=0, transcendentals=0),
            name="plan",
        )(graph_count, slot_table, sink_table)
        pairs_for = pl.pallas_call(
            zip_kernel,
            out_shape=[pltpu.VMEM((2,) + slab, BF16)] * half,
            in_specs=[VMEM] * 3,
            out_specs=[VMEM] * half,
            compiler_params=params(16),
            name="zip",
        )(mine, got, table)
        arrived = {0: pairs_for[0]}
        for i in order:
            arrived[i] = xor_permute(pairs_for[i], readers, 2 * i)
        rows = readers * sinks + 1
        factors, early_sum = pl.pallas_call(
            functools.partial(early_kernel, STEP, root_scale, early),
            out_shape=[
                pltpu.VMEM((rows,) + slab, BF16),
                pltpu.VMEM((evecs, 2 * evecs), F32),
            ],
            in_specs=[VMEM] * (2 + len(early)),
            out_specs=[VMEM] * 2,
            scratch_shapes=[
                pltpu.SMEM((8, graphs + LANES), jnp.int32),
                pltpu.SemaphoreType.DMA,
            ],
            compiler_params=params(16),
            cost_estimate=pl.CostEstimate(
                flops=8 * len(early) * sinks * evecs**3, bytes_accessed=0, transcendentals=0
            ),
            name="early",
        )(table, resident, *[arrived[i] for i in early])
        edge, _ = pl.pallas_call(
            functools.partial(late_kernel, STEP, root_scale, edge_scale, late),
            out_shape=[
                pltpu.VMEM((1,) + slab, BF16),
                pltpu.VMEM((rows,) + slab, BF16),
            ],
            in_specs=[VMEM] * (4 + len(late)),
            out_specs=[VMEM] * 2,
            scratch_shapes=[
                pltpu.SMEM((8, graphs + LANES), jnp.int32),
                pltpu.SemaphoreType.DMA,
            ],
            input_output_aliases={3 + len(late): 1},
            compiler_params=params(16),
            name="edge",
        )(table, early_sum, resident, *[arrived[i] for i in late], factors)
    else:
        outgoing = pl.pallas_call(
            rotate_kernel,
            out_shape=jax.ShapeDtypeStruct((readers,) + slab, BF16),
            in_specs=[HBM] * 3,
            out_specs=VMEM,
            scratch_shapes=rotate_scratch,
            compiler_params=params(24),
            name="rotate",
        )(*rotate_args)
        received = lax.all_to_all(outgoing, "had", split_axis=0, concat_axis=0, tiled=True)
        edge = pl.pallas_call(
            functools.partial(edge_kernel, block, root_scale, edge_scale),
            out_shape=jax.ShapeDtypeStruct((1,) + slab, BF16),
            in_specs=[SMEM, SMEM, SMEM, VMEM, VMEM],
            out_specs=VMEM,
            scratch_shapes=[pltpu.VMEM((readers * sinks + 1,) + slab, BF16)] if dense else [],
            compiler_params=params(32),
            name="edge",
        )(*counts, received, sink_slabs)

    parts, place = gather_edges(edge, readers)
    pair_products = pl.pallas_call(
        functools.partial(pair_kernel, root_scale, place),
        out_shape=jax.ShapeDtypeStruct((pairs,) + slab, BF16),
        in_specs=[SMEM] + [VMEM] * len(parts),
        out_specs=HBM,
        scratch_shapes=[
            pltpu.VMEM((readers,) + slab, BF16),
            pltpu.VMEM((pairs,) + slab, BF16),
            pltpu.SemaphoreType.DMA((pairs,)),
        ],
        compiler_params=params(24),
        name="pairs",
    )(pair_list.T, *parts)
    return edge, pair_products


def solution(mesh):
    return jax.shard_map(
        functools.partial(shards, mesh.shape["had"]),
        mesh=mesh,
        in_specs=(
            P(("grp", "had"), None, None),
            P(("grp", "had"), None, None),
            P("grp", None, None, None),
            P(("grp", "had"), None),
            P(("grp", "had"), None, None),
            P(("grp", "had"), None, None),
            P(("grp", "had")),
            P(("grp", "had"), None),
        ),
        out_specs=(P(("grp", "had"), None, None), P(("grp", "had"), None, None)),
        check_vma=False,
    )
```
